256 devices in a mesh: tm: 32 (over y, z), tile: 8 (over x, core).
Axes of the slice: x: 4, y: 4, z: 8, core: 2. Of those that a mesh axis runs over, the one named last changes fastest.
Arguments:
- features: bfloat16 [256, 2, 256, 256], P('tile', None, 'tm'), may hold values from -6 to 6
- cotangent: bfloat16 [256, 2, 256, 256], P('tile', None, 'tm'), may hold values from -6 to 6
- valid_dates: int32 [256, 256], P('tile', 'tm'), may hold values from 0 to 1, as said below
- gain_first: float32 [256], replicated, may hold values from 0.1 to 1.9
- qkv_weight: bfloat16 [256, 768], replicated, may hold values from -0.75625 to 0.75625
- out_weight: bfloat16 [256, 256], replicated, may hold values from -0.375 to 0.375
- gain_second: float32 [256], replicated, may hold values from 0.1 to 1.9
- up_weight: bfloat16 [256, 1024], replicated, may hold values from -0.375 to 0.375
- down_weight: bfloat16 [1024, 256], replicated, may hold values from -0.1875 to 0.1875
Outputs:
- feature_grad: bfloat16 [256, 2, 256, 256], P('tile', None, 'tm')
- qkv_grad: float32 [256, 768], replicated
- out_grad: float32 [256, 256], replicated
- up_grad: float32 [256, 1024], replicated
- down_grad: float32 [1024, 256], replicated
The draws below stay inside these ranges and needn't reach their ends.
Inputs may be any that keep to these rules, and one draw needn't show every extreme that they name: `valid_dates`: for every block and every index of tm, between 1 and 4 of the 8 dates that this index holds are valid; in every tile group some block has exactly 4 valid dates on every index of tm.
All inputs are finite; a program needn't handle non-finite values.
Results may differ from the reference program's by a relative error of at most 0.01.
The reference program's roundings to bfloat16 on the way count: a program that leaves them out, or rounds other values in their place, can miss the bound.
Values may be sent and summed in bfloat16 or wider, within the bound.
No kernel may reach another device: no remote copies, remote signals or barrier semaphores. Data moves between devices by JAX's collectives and lax.ppermute only.
A program may use at most 64 MiB of HBM per device.

```python
import jax
import jax.numpy as jnp
from jax import lax

D = 256
HEADS = 16
FF = 1024
PIX = 2
DATE_DEV = 8
CAP = 4
BLK_TILE = 32
NBLK = 256
NDATE = 256
N_TM = 32


def draw_valid_dates(key, part):
    keys = jax.random.split(key, 4)
    group_count = NBLK // BLK_TILE
    level = jax.random.randint(keys[0], (NBLK, 1), 1, CAP + 1)
    raw_draw = jax.random.randint(keys[1], (NBLK, N_TM), 0, 1 << 20)
    counts = 1 + raw_draw % level
    heavy = jax.random.randint(keys[2], (group_count, 1), 0, BLK_TILE)
    local_ids = lax.broadcasted_iota(jnp.int32, (group_count, BLK_TILE), 1)
    full_rows = (local_ids == heavy).reshape(NBLK, 1)
    counts = jnp.where(full_rows, CAP, counts)
    ranked = jax.random.randint(keys[3], (NBLK, N_TM, DATE_DEV), 0, 1 << 16) * DATE_DEV + lax.broadcasted_iota(jnp.int32, (NBLK, N_TM, DATE_DEV), 2)
    ordering = jnp.argsort(ranked, axis=-1, stable=True)
    position = jnp.argsort(ordering, axis=-1, stable=True)
    chosen = position < counts[:, :, None]
    return chosen.reshape(NBLK, NDATE).astype(jnp.int32)


def draw_qkv_weight(key, part):
    first_key = jax.random.fold_in(key, 0)
    base = jnp.clip(jax.random.normal(first_key, (D, 3 * D), jnp.float32), -4.0, 4.0) * float(D) ** (-0.5)
    return base.astype(jnp.bfloat16)


def block_levels(rng, dims, cuts, low, top_value):
    def one(axis_at, blocks):
        steps = jax.random.uniform(jax.random.fold_in(jax.random.fold_in(rng, 6), axis_at), (blocks,), jnp.float32, low / len(cuts), top_value / len(cuts))
        return jnp.repeat(jnp.exp(steps), dims[axis_at] // blocks).reshape((-1,) + (1,) * (len(dims) - axis_at - 1))

    level = one(*cuts[0])
    for cut in cuts[1:]:
        level = level * one(*cut)
    return level


def gaussian(rng, dims, spread, bound, shards=(), held_as=jnp.bfloat16):
    entries = spread * jax.random.normal(rng, dims, jnp.float32)
    if shards:
        entries = entries * block_levels(rng, dims, shards, -0.22, 0.18)
    return jnp.clip(entries, -bound, bound).astype(held_as)


def setup_inputs(seed: int = 0) -> dict:
    seeds = jax.random.split(jax.random.key(seed), 10)
    features = gaussian(seeds[0], (NBLK, PIX, NDATE, D), 1.0, 6.0, ((0, 8), (2, 32)))
    cotangent = gaussian(seeds[1], (NBLK, PIX, NDATE, D), 1.0, 6.0, ((0, 8), (2, 32)))
    valid_dates = draw_valid_dates(jax.random.fold_in(seeds[9], 71), 0)
    gain_first = jnp.clip(1.0 + 0.18 * jax.random.normal(seeds[3], (D,), jnp.float32), 0.1, 1.9)
    qkv_weight = draw_qkv_weight(jax.random.fold_in(seeds[9], 71), 0)
    out_weight = gaussian(seeds[5], (D, D), D ** -0.5, 0.375)
    gain_second = jnp.clip(1.0 + 0.18 * jax.random.normal(seeds[6], (D,), jnp.float32), 0.1, 1.9)
    up_weight = gaussian(seeds[7], (D, FF), D ** -0.5, 0.375)
    down_weight = gaussian(seeds[8], (FF, D), FF ** -0.5, 0.1875)
    return dict(features=features, cotangent=cotangent, valid_dates=valid_dates, gain_first=gain_first, qkv_weight=qkv_weight, out_weight=out_weight, gain_second=gain_second, up_weight=up_weight, down_weight=down_weight)


EPS = 1e-05
GELU_C = 0.7978845608028654
GELU_A = 0.044715

def gelu_tanh(inputs):
    inner = GELU_C * (inputs + GELU_A * inputs * inputs * inputs)
    return 0.5 * inputs * (1.0 + jnp.tanh(inner))

def gelu_slope(inputs):
    inner = GELU_C * (inputs + GELU_A * inputs * inputs * inputs)
    tangent = jnp.tanh(inner)
    return 0.5 * (1.0 + tangent) + 0.5 * inputs * (1.0 - tangent * tangent) * GELU_C * (1.0 + 3.0 * GELU_A * inputs * inputs)

def norm_rows(hidden):
    centre = hidden - lax.optimization_barrier(jnp.mean(hidden, axis=-1, keepdims=True))
    inverse = lax.rsqrt(lax.optimization_barrier(jnp.mean(centre * centre, axis=-1, keepdims=True)) + EPS)
    return (centre * inverse, inverse)

def norm_back(normed, inverse, gain, upstream):
    scaled = upstream * gain
    return inverse * (scaled - lax.optimization_barrier(jnp.mean(scaled, axis=-1, keepdims=True)) - normed * lax.optimization_barrier(jnp.mean(scaled * normed, axis=-1, keepdims=True)))

def outer_rows(left, right):
    return jnp.dot(left.T, right, preferred_element_type=jnp.float32)

def back_dot(left, weight):
    return jnp.dot(left, weight.T, preferred_element_type=jnp.float32)

def mix_heads(form, left, right):
    return jnp.einsum(form, left.astype(jnp.float32), right.astype(jnp.float32))

def masked_scores(query_blk, key_blk, keep_row, factor):
    scores = mix_heads('lhe,mhe->hlm', query_blk, key_blk) * factor
    return jnp.where(keep_row[None, None, :] > 0, scores, -1e+30)

def layer_backward(features, cotangent, keep_mask, gain_first, qkv_weight, out_weight, gain_second, up_weight, down_weight, head_count):
    seq_count, length, model_width = features.shape
    head_dim = model_width // head_count
    factor = float(head_dim) ** (-0.5)
    row_count = seq_count * length
    keep_col = keep_mask.reshape(row_count, 1).astype(jnp.float32)
    inputs = features.reshape(row_count, model_width).astype(jnp.float32)
    upstream = (cotangent.reshape(row_count, model_width).astype(jnp.float32) * keep_col).astype(jnp.bfloat16)
    normed_one, inverse_one = norm_rows(inputs)
    first_in = (normed_one * gain_first).astype(jnp.bfloat16)
    projected = jnp.dot(first_in, qkv_weight, preferred_element_type=jnp.float32).astype(jnp.bfloat16)
    projected = projected.reshape(seq_count, length, 3, head_count, head_dim)
    queries = projected[:, :, 0]
    key_rows = projected[:, :, 1]
    value_rows = projected[:, :, 2]

    def attend_block(pieces):
        query_blk, key_blk, value_blk, keep_row = pieces
        scores = masked_scores(query_blk, key_blk, keep_row, factor)
        highest = lax.optimization_barrier(jnp.max(scores, axis=-1, keepdims=True))
        powered = jnp.exp(scores - highest)
        denominator = lax.optimization_barrier(jnp.sum(powered, axis=-1, keepdims=True))
        attn_probs = (powered / denominator).astype(jnp.bfloat16)
        attended = mix_heads('hlm,mhe->lhe', attn_probs, value_blk).astype(jnp.bfloat16)
        return (attended, highest, denominator)
    attended, highest, denominator = lax.map(attend_block, (queries, key_rows, value_rows, keep_mask))
    attended_rows = attended.reshape(row_count, model_width)
    residual = inputs + jnp.dot(attended_rows, out_weight, preferred_element_type=jnp.float32)
    normed_two, inverse_two = norm_rows(residual)
    second_in = (normed_two * gain_second).astype(jnp.bfloat16)
    pre_act = jnp.dot(second_in, up_weight, preferred_element_type=jnp.float32)
    activated = gelu_tanh(pre_act).astype(jnp.bfloat16)
    down_grad = outer_rows(activated, upstream)
    hidden_grad = (back_dot(upstream, down_weight) * gelu_slope(pre_act)).astype(jnp.bfloat16)
    up_grad = outer_rows(second_in, hidden_grad)
    resid_grad = upstream.astype(jnp.float32) + norm_back(normed_two, inverse_two, gain_second, back_dot(hidden_grad, up_weight))
    resid_half = resid_grad.astype(jnp.bfloat16)
    out_grad = outer_rows(attended_rows, resid_half)
    attended_grad = back_dot(resid_half, out_weight).astype(jnp.bfloat16).reshape(seq_count, length, head_count, head_dim)

    def attend_back(pieces):
        query_blk, key_blk, value_blk, keep_row, highest_blk, denom_blk, grad_blk = pieces
        scores = masked_scores(query_blk, key_blk, keep_row, factor)
        attn_full = jnp.exp(scores - highest_blk) / denom_blk
        attn_probs = attn_full.astype(jnp.bfloat16)
        prob_grad = mix_heads('lhe,mhe->hlm', grad_blk, value_blk)
        score_grad = (attn_full * (prob_grad - lax.optimization_barrier(jnp.sum(attn_full * prob_grad, axis=-1, keepdims=True))) * factor).astype(jnp.bfloat16)
        query_grad = mix_heads('hlm,mhe->lhe', score_grad, key_blk)
        key_grad = mix_heads('hlm,lhe->mhe', score_grad, query_blk)
        value_grad = mix_heads('hlm,lhe->mhe', attn_probs, grad_blk)
        return jnp.stack([query_grad, key_grad, value_grad], axis=1).astype(jnp.bfloat16)
    proj_grad = lax.map(attend_back, (queries, key_rows, value_rows, keep_mask, highest, denominator, attended_grad))
    proj_grad = proj_grad.reshape(row_count, 3 * model_width)
    qkv_grad = outer_rows(first_in, proj_grad)
    feature_grad = (resid_grad + norm_back(normed_one, inverse_one, gain_first, back_dot(proj_grad, qkv_weight))) * keep_col
    feature_grad = feature_grad.astype(jnp.bfloat16).reshape(seq_count, length, model_width)
    return (feature_grad, (qkv_grad, out_grad, up_grad, down_grad))

def reference(features, cotangent, valid_dates, gain_first, qkv_weight, out_weight, gain_second, up_weight, down_weight):
    grad_scale = float(NBLK * PIX * NDATE) ** (-0.5)
    keep_all = valid_dates.astype(jnp.bfloat16)

    def one_block(carry, pieces):
        block_feat, block_cot, block_keep = pieces
        keep_mask = jnp.broadcast_to(block_keep[None, :], (PIX, NDATE))
        block_grad, partials = layer_backward(block_feat, block_cot, keep_mask, gain_first, qkv_weight, out_weight, gain_second, up_weight, down_weight, HEADS)
        return (jax.tree.map(jnp.add, carry, partials), block_grad)
    start = (jnp.zeros((D, 3 * D), jnp.float32), jnp.zeros((D, D), jnp.float32), jnp.zeros((D, FF), jnp.float32), jnp.zeros((FF, D), jnp.float32))
    totals, feature_grad = lax.scan(one_block, start, (features, cotangent, keep_all))
    qkv_grad, out_grad, up_grad, down_grad = totals
    return (feature_grad, qkv_grad * grad_scale, out_grad * grad_scale, up_grad * grad_scale, down_grad * grad_scale)
```

```python
import functools

import jax
import jax.numpy as jnp
from jax import lax
from jax.experimental import pallas as pl
from jax.experimental.pallas import tpu as pltpu
from jax.sharding import Mesh
from jax.sharding import PartitionSpec as P

HEADS = 16
CAP = 4
EPS = 1e-05
GELU_C = 0.7978845608028654
GELU_A = 0.044715
ABSENT = 2.0**100

F32 = jnp.float32
BF16 = jnp.bfloat16
VMEM_LIMIT = 48 * 1024 * 1024


def iota(shape, axis):
    return lax.broadcasted_iota(jnp.int32, shape, axis)


def dot(left, right, dims=((1,), (0,))):
    return lax.dot_general(left, right, (dims, ((), ())), preferred_element_type=F32)


TN = ((0,), (0,))
NT = ((1,), (1,))


def slot_matrix(valid, group, rows_per_block):
    date = iota((8, 256), 1) % 8
    day = iota((8, 256), 0)
    held = valid[group * 16 : group * 16 + 16, :].astype(F32)
    keep_all = dot(held, (day == date).astype(F32))
    rank_all = dot(held, (day < date).astype(F32))
    own = iota((16, 256), 0) == iota((16, 256), 1) // 16
    keep = jnp.sum(jnp.where(own, keep_all, 0.0), axis=0, keepdims=True)
    rank = jnp.sum(jnp.where(own, rank_all, 0.0), axis=0, keepdims=True)
    shape = (16 * rows_per_block, 256)
    row, col = iota(shape, 0), iota(shape, 1)
    match = (
        (row // rows_per_block == col // 16)
        & ((row // 4) % 2 == (col // 8) % 2)
        & (rank == (row % 4).astype(F32))
        & (keep > 0.5)
    )
    return match.astype(F32)


def compact_kernel(feat_ref, cot_ref, valid_ref, send_ref):
    valid = valid_ref[...]
    for group in range(2):
        match = slot_matrix(valid, group, 16)
        is_feat = (iota((256, 1), 0) // 8) % 2 == 0
        pick_feat = jnp.where(is_feat, match, 0.0).astype(BF16)
        pick_cot = jnp.where(is_feat, 0.0, match).astype(BF16)
        rows = pl.ds(group * 256, 256)
        got = dot(pick_feat, feat_ref[rows, :]) + dot(pick_cot, cot_ref[rows, :])
        filled = jnp.sum(match, axis=1, keepdims=True) > 0.5
        got = jnp.where(is_feat & jnp.logical_not(filled), ABSENT, got)
        send_ref[rows, :] = got.astype(BF16)


def expand_kernel(back_ref, valid_ref, out_ref):
    valid = valid_ref[...]
    for group in range(2):
        match = slot_matrix(valid, group, 8).astype(BF16)
        back = back_ref[pl.ds(group * 128, 128), :]
        out_ref[pl.ds(group * 256, 256), :] = dot(match, back, TN).astype(BF16)


def row_mean(values):
    return jnp.sum(values, axis=-1, keepdims=True) * (1.0 / values.shape[-1])


def norm_rows(hidden):
    centre = hidden - row_mean(hidden)
    inverse = lax.rsqrt(row_mean(centre * centre) + EPS)
    return centre * inverse, inverse


def norm_back(normed, inverse, gain, upstream):
    scaled = upstream * gain
    return inverse * (scaled - row_mean(scaled) - normed * row_mean(scaled * normed))


def layer_kernel(
    scale,
    recv_ref,
    gain_first_ref,
    qkv_ref,
    out_w_ref,
    gain_second_ref,
    up_ref,
    down_ref,
    grad_ref,
    terms_ref,
    probs,
    proj_t,
    att_t,
    att_grad_t,
    proj_grad_t,
):
    core = lax.axis_index("c")

    def put(group, columns, value):
        terms_ref[(group % 2) ^ core, group // 2, :, columns] = (value * scale).astype(BF16)

    token = iota((256, 512), 0)
    target = (token % 128) // 4 * 16 + token // 128 * 4 + token % 4
    source = iota((256, 512), 1)
    recv = recv_ref[...]
    inputs = dot((source == target).astype(BF16), recv)
    upstream = dot((source == target + 8).astype(BF16), recv).astype(BF16)
    keep = inputs[:, 0:1] < 0.5 * ABSENT
    inputs = jnp.where(keep, inputs, 0.0)
    gain_first = gain_first_ref[...]
    gain_second = gain_second_ref[...]

    normed_one, inverse_one = norm_rows(inputs)
    first_in = (normed_one * gain_first).astype(BF16)
    proj_t[...] = dot(qkv_ref[...], first_in, ((0,), (1,))).astype(BF16)

    def attend(head, carry):
        at = pl.multiple_of(head * 16, 16)
        for pix in range(2):
            cols = pl.ds(pix * 128, 128)
            query = proj_t[pl.ds(at, 16), cols]
            key = proj_t[pl.ds(256 + at, 16), cols]
            value = proj_t[pl.ds(512 + at, 16), cols]
            scores = dot(key, query, TN) * 0.25
            scores = jnp.where(keep[pix * 128 : pix * 128 + 128], scores, -1e30)
            powered = jnp.exp(scores - jnp.max(scores, axis=0, keepdims=True))
            full = powered * (1.0 / jnp.sum(powered, axis=0, keepdims=True))
            probs[pix, head] = full
            att_t[pl.ds(at, 16), cols] = dot(value, full.astype(BF16)).astype(BF16)
        return carry

    lax.fori_loop(0, HEADS, attend, 0, unroll=4)

    attended_t = att_t[...]
    out_w = out_w_ref[...]
    residual = inputs + dot(attended_t, out_w, TN)
    normed_two, inverse_two = norm_rows(residual)
    second_in = (normed_two * gain_second).astype(BF16)
    back = jnp.zeros((256, 256), F32)
    for part in range(4):
        cols = pl.ds(part * 256, 256)
        up_part = up_ref[:, cols]
        pre = dot(second_in, up_part)
        tangent = jnp.tanh(GELU_C * (pre + GELU_A * pre * pre * pre))
        activated = (0.5 * pre * (1.0 + tangent)).astype(BF16)
        slope = 0.5 * (1.0 + tangent) + 0.5 * pre * (1.0 - tangent * tangent) * GELU_C * (
            1.0 + 3.0 * GELU_A * pre * pre
        )
        put(4 + part, slice(0, 256), dot(activated, upstream, TN))
        hidden_grad = (dot(upstream, down_ref[cols, :], NT) * slope).astype(BF16)
        put(part, slice(0, 256), dot(second_in, hidden_grad, TN))
        back = back + dot(hidden_grad, up_part, NT)
    resid_grad = upstream.astype(F32) + norm_back(normed_two, inverse_two, gain_second, back)
    resid_half = resid_grad.astype(BF16)
    out_grad = dot(attended_t, resid_half)
    put(6, slice(256, 384), out_grad[:, :128])
    put(7, slice(256, 384), out_grad[:, 128:])
    att_grad_t[...] = dot(out_w, resid_half, NT).astype(BF16)

    def attend_back(head, carry):
        at = pl.multiple_of(head * 16, 16)
        for pix in range(2):
            cols = pl.ds(pix * 128, 128)
            query = proj_t[pl.ds(at, 16), cols]
            key = proj_t[pl.ds(256 + at, 16), cols]
            value = proj_t[pl.ds(512 + at, 16), cols]
            grad = att_grad_t[pl.ds(at, 16), cols]
            full = probs[pix, head]
            prob_grad = dot(value, grad, TN)
            total = jnp.sum(full * prob_grad, axis=0, keepdims=True)
            score_grad = (full * (prob_grad - total) * 0.25).astype(BF16)
            proj_grad_t[pl.ds(at, 16), cols] = dot(key, score_grad).astype(BF16)
            proj_grad_t[pl.ds(256 + at, 16), cols] = dot(query, score_grad, NT).astype(BF16)
            proj_grad_t[pl.ds(512 + at, 16), cols] = dot(grad, full.astype(BF16), NT).astype(BF16)
        return carry

    lax.fori_loop(0, HEADS, attend_back, 0, unroll=4)

    grad_t = proj_grad_t[...]
    first_t = first_in.T
    for part in range(3):
        qkv_grad = dot(first_t, grad_t[part * 256 : part * 256 + 256], NT)
        put(2 * part, slice(256, 384), qkv_grad[:, :128])
        put(2 * part + 1, slice(256, 384), qkv_grad[:, 128:])
    first_back = dot(grad_t, qkv_ref[...], ((0,), (1,)))
    grad = resid_grad + norm_back(normed_one, inverse_one, gain_first, first_back)
    grad = jnp.where(keep, grad, 0.0).astype(BF16)
    slot = iota((256, 256), 0)
    want = slot // 4 % 2 * 128 + slot // 8 * 4 + slot % 4
    grad_ref[...] = dot((iota((256, 256), 1) == want).astype(BF16), grad).astype(BF16)


def spread_kernel(mine_ref, other_ref, qkv_ref, out_ref, up_ref, down_ref):
    core = lax.axis_index("c")
    for group in range(8):
        flip = (group % 2) ^ core
        near, far = mine_ref[group // 2], other_ref[group // 2]
        piece = jnp.where(flip == 0, near.astype(F32), far.astype(F32))
        if group < 4:
            up_ref[:, pl.ds(group * 256, 256)] = piece[:, :256]
        else:
            down_ref[pl.ds((group - 4) * 256, 256), :] = piece[:, :256]
        if group < 6:
            qkv_ref[:, pl.ds(group * 128, 128)] = piece[:, 256:]
        else:
            out_ref[:, pl.ds((group - 6) * 128, 128)] = piece[:, 256:]


def run(kernel, out_shape, *args, scratch=()):
    return pl.pallas_call(
        kernel,
        out_shape=out_shape,
        scratch_shapes=list(scratch),
        compiler_params=pltpu.CompilerParams(vmem_limit_bytes=VMEM_LIMIT),
    )(*args)


def sum_leading(parts):
    return jnp.sum(parts.astype(F32), axis=0).astype(BF16)


def per_device(
    features,
    cotangent,
    valid_dates,
    gain_first,
    qkv_weight,
    out_weight,
    gain_second,
    up_weight,
    down_weight,
):
    shape = jax.ShapeDtypeStruct
    width = features.shape[-1]
    scale = float(256 * 2 * 256) ** (-0.5)
    with jax.named_scope("compact"):
        send = run(
            compact_kernel,
            shape((512, width), BF16),
            features.reshape(512, width),
            cotangent.reshape(512, width),
            valid_dates,
        )
    with jax.named_scope("to_owner"):
        recv = lax.all_to_all(
            send.reshape(32, 16, width), ("y", "z"), split_axis=0, concat_axis=0, tiled=True
        )
    with jax.named_scope("layer"):
        grad, terms = run(
            functools.partial(layer_kernel, scale),
            (shape((256, width), BF16), shape((2, 4, 256, 384), BF16)),
            recv.reshape(512, width),
            gain_first.reshape(1, width),
            qkv_weight,
            out_weight,
            gain_second.reshape(1, width),
            up_weight,
            down_weight,
            scratch=(
                pltpu.VMEM((2, HEADS, 128, 128), F32),
                pltpu.VMEM((768, 256), BF16),
                pltpu.VMEM((256, 256), BF16),
                pltpu.VMEM((256, 256), BF16),
                pltpu.VMEM((768, 256), BF16),
            ),
        )
    with jax.named_scope("core_sum"):
        other = lax.ppermute(terms[1], "c", [(0, 1), (1, 0)])
        halves = (terms[0].astype(F32) + other.astype(F32)).astype(BF16)
    with jax.named_scope("x_sum"):
        halves = lax.all_to_all(halves, "x", split_axis=0, concat_axis=0, tiled=True)
        part = sum_leading(halves)
    with jax.named_scope("yz_sum"):
        joint = jnp.concatenate(
            [part.reshape(32, 8, 384), grad.reshape(32, 8, width)], axis=2
        )
        joint = lax.all_to_all(joint, ("y", "z"), split_axis=0, concat_axis=0, tiled=True)
        total = sum_leading(joint[:, :, :384])
        back = joint[:, :, 384:]
    with jax.named_scope("yz_gather"):
        part = lax.all_to_all(
            jnp.broadcast_to(total[None], (32, 8, 384)),
            ("y", "z"),
            split_axis=0,
            concat_axis=0,
            tiled=True,
        ).reshape(256, 384)
    with jax.named_scope("x_gather"):
        mine = lax.all_gather(part, "x", axis=0)
    with jax.named_scope("core_gather"):
        other = lax.ppermute(mine, "c", [(0, 1), (1, 0)])
    with jax.named_scope("spread"):
        outs = run(
            spread_kernel,
            (
                shape((256, 768), F32),
                shape((256, 256), F32),
                shape((256, 1024), F32),
                shape((1024, 256), F32),
            ),
            mine,
            other,
        )
    with jax.named_scope("expand"):
        feature_grad = run(
            expand_kernel, shape((512, width), BF16), back.reshape(256, width), valid_dates
        )
    return (feature_grad.reshape(features.shape), *outs)


def solution(mesh):
    fine = Mesh(mesh.devices.reshape(4, 8, 4, 2), ("y", "z", "x", "c"))
    dates, tiles = ("y", "z"), ("x", "c")
    in_specs = (
        P(tiles, None, dates, None),
        P(tiles, None, dates, None),
        P(tiles, dates),
        P(),
        P(),
        P(),
        P(),
        P(),
        P(),
    )
    out_specs = (P(tiles, None, dates, None), P(), P(), P(), P())
    return jax.shard_map(
        per_device, mesh=fine, in_specs=in_specs, out_specs=out_specs, check_vma=False
    )
```

```python
import functools

import jax
import jax.numpy as jnp
from jax import lax
from jax.experimental import pallas as pl
from jax.experimental.pallas import tpu as pltpu
from jax.sharding import Mesh
from jax.sharding import PartitionSpec as P

HEADS = 16
CAP = 4
EPS = 1e-05
GELU_C = 0.7978845608028654
GELU_A = 0.044715
ABSENT = 2.0**100

F32 = jnp.float32
BF16 = jnp.bfloat16
VMEM_LIMIT = 48 * 1024 * 1024


def iota(shape, axis):
    return lax.broadcasted_iota(jnp.int32, shape, axis)


def dot(left, right, dims=((1,), (0,))):
    return lax.dot_general(left, right, (dims, ((), ())), preferred_element_type=F32)


TN = ((0,), (0,))
NT = ((1,), (1,))


def slot_matrix(valid, group, rows_per_block):
    date = iota((8, 256), 1) % 8
    day = iota((8, 256), 0)
    held = valid[group * 16 : group * 16 + 16, :].astype(F32)
    keep_all = dot(held, (day == date).astype(F32))
    rank_all = dot(held, (day < date).astype(F32))
    own = iota((16, 256), 0) == iota((16, 256), 1) // 16
    keep = jnp.sum(jnp.where(own, keep_all, 0.0), axis=0, keepdims=True)
    rank = jnp.sum(jnp.where(own, rank_all, 0.0), axis=0, keepdims=True)
    shape = (16 * rows_per_block, 256)
    row, col = iota(shape, 0), iota(shape, 1)
    match = (
        (row // rows_per_block == col // 16)
        & ((row // 4) % 2 == (col // 8) % 2)
        & (rank == (row % 4).astype(F32))
        & (keep > 0.5)
    )
    return match.astype(F32)


def compact_kernel(feat_hbm, cot_hbm, valid_ref, send_ref, feat, cot, arrived):
    copies = []
    for group in range(2):
        rows = pl.ds(group * 256, 256)
        copies.append(
            [
                pltpu.make_async_copy(feat_hbm.at[rows], feat.at[rows], arrived.at[group, 0]),
                pltpu.make_async_copy(cot_hbm.at[rows], cot.at[rows], arrived.at[group, 1]),
            ]
        )
    for pair in copies:
        for copy in pair:
            copy.start()
    valid = valid_ref[...]
    for group in range(2):
        match = slot_matrix(valid, group, 16)
        is_feat = (iota((256, 1), 0) // 8) % 2 == 0
        pick_feat = jnp.where(is_feat, match, 0.0).astype(BF16)
        pick_cot = jnp.where(is_feat, 0.0, match).astype(BF16)
        filled = jnp.sum(match, axis=1, keepdims=True) > 0.5
        rows = pl.ds(group * 256, 256)
        for copy in copies[group]:
            copy.wait()
        got = dot(pick_feat, feat[rows, :]) + dot(pick_cot, cot[rows, :])
        got = jnp.where(is_feat & jnp.logical_not(filled), ABSENT, got)
        send_ref[rows, :] = got.astype(BF16)


def row_mean(values):
    return jnp.sum(values, axis=-1, keepdims=True) * (1.0 / values.shape[-1])


def norm_rows(hidden):
    centre = hidden - row_mean(hidden)
    inverse = lax.rsqrt(row_mean(centre * centre) + EPS)
    return centre * inverse, inverse


def norm_back(normed, inverse, gain, upstream):
    scaled = upstream * gain
    return inverse * (scaled - row_mean(scaled) - normed * row_mean(scaled * normed))


def layer_kernel(
    scale,
    recv_ref,
    gain_first_hbm,
    qkv_hbm,
    out_w_hbm,
    gain_second_hbm,
    up_hbm,
    down_hbm,
    grad_ref,
    mine_ref,
    theirs_ref,
    gain_first_ref,
    qkv_ref,
    out_w_ref,
    gain_second_ref,
    up_ref,
    down_ref,
    arrived,
    probs,
    proj_t,
    att_t,
    att_grad_t,
    proj_grad_t,
):
    copies = [
        pltpu.make_async_copy(held, ref, arrived.at[at])
        for at, (held, ref) in enumerate(
            (
                (gain_first_hbm, gain_first_ref),
                (qkv_hbm, qkv_ref),
                (out_w_hbm, out_w_ref),
                (gain_second_hbm, gain_second_ref),
                (up_hbm, up_ref),
                (down_hbm, down_ref),
            )
        )
    ]
    for copy in copies:
        copy.start()
    core = lax.axis_index("c")
    place = lax.axis_index("x")

    def put(group, columns, value):
        slot = lax.rem(group // 2 - place + 4, 4)
        value = (value * scale).astype(BF16)

        @pl.when(core == group % 2)
        def _():
            mine_ref[slot, :, columns] = value

        @pl.when(core != group % 2)
        def _():
            theirs_ref[slot, :, columns] = value

    token = iota((256, 512), 0)
    target = (token % 128) // 4 * 16 + token // 128 * 4 + token % 4
    source = iota((256, 512), 1)
    recv = recv_ref[...]
    inputs = dot((source == target).astype(BF16), recv)
    upstream = dot((source == target + 8).astype(BF16), recv).astype(BF16)
    keep = inputs[:, 0:1] < 0.5 * ABSENT
    inputs = jnp.where(keep, inputs, 0.0)
    copies[0].wait()
    copies[1].wait()
    gain_first = gain_first_ref[...]

    normed_one, inverse_one = norm_rows(inputs)
    first_in = (normed_one * gain_first).astype(BF16)
    proj_t[...] = dot(qkv_ref[...], first_in, ((0,), (1,))).astype(BF16)

    def attend(head, carry):
        at = pl.multiple_of(head * 16, 16)
        for pix in range(2):
            cols = pl.ds(pix * 128, 128)
            query = proj_t[pl.ds(at, 16), cols]
            key = proj_t[pl.ds(256 + at, 16), cols]
            value = proj_t[pl.ds(512 + at, 16), cols]
            scores = dot(key, query, TN) * 0.25
            scores = jnp.where(keep[pix * 128 : pix * 128 + 128], scores, -1e30)
            powered = jnp.exp(scores - jnp.max(scores, axis=0, keepdims=True))
            full = powered * (1.0 / jnp.sum(powered, axis=0, keepdims=True))
            probs[pix, head] = full
            att_t[pl.ds(at, 16), cols] = dot(value, full.astype(BF16)).astype(BF16)
        return carry

    lax.fori_loop(0, HEADS, attend, 0, unroll=4)

    for copy in copies[2:]:
        copy.wait()
    gain_second = gain_second_ref[...]
    attended_t = att_t[...]
    out_w = out_w_ref[...]
    residual = inputs + dot(attended_t, out_w, TN)
    normed_two, inverse_two = norm_rows(residual)
    second_in = (normed_two * gain_second).astype(BF16)
    back = jnp.zeros((256, 256), F32)
    for part in range(4):
        cols = pl.ds(part * 256, 256)
        up_part = up_ref[:, cols]
        pre = dot(second_in, up_part)
        tangent = jnp.tanh(GELU_C * (pre + GELU_A * pre * pre * pre))
        activated = (0.5 * pre * (1.0 + tangent)).astype(BF16)
        slope = 0.5 * (1.0 + tangent) + 0.5 * pre * (1.0 - tangent * tangent) * GELU_C * (
            1.0 + 3.0 * GELU_A * pre * pre
        )
        put(4 + part, slice(0, 256), dot(activated, upstream, TN))
        hidden_grad = (dot(upstream, down_ref[cols, :], NT) * slope).astype(BF16)
        put(part, slice(0, 256), dot(second_in, hidden_grad, TN))
        back = back + dot(hidden_grad, up_part, NT)
    resid_grad = upstream.astype(F32) + norm_back(normed_two, inverse_two, gain_second, back)
    resid_half = resid_grad.astype(BF16)
    out_grad = dot(attended_t, resid_half)
    put(6, slice(256, 384), out_grad[:, :128])
    put(7, slice(256, 384), out_grad[:, 128:])
    att_grad_t[...] = dot(out_w, resid_half, NT).astype(BF16)

    def attend_back(head, carry):
        at = pl.multiple_of(head * 16, 16)
        for pix in range(2):
            cols = pl.ds(pix * 128, 128)
            query = proj_t[pl.ds(at, 16), cols]
            key = proj_t[pl.ds(256 + at, 16), cols]
            value = proj_t[pl.ds(512 + at, 16), cols]
            grad = att_grad_t[pl.ds(at, 16), cols]
            full = probs[pix, head]
            prob_grad = dot(value, grad, TN)
            total = jnp.sum(full * prob_grad, axis=0, keepdims=True)
            score_grad = (full * (prob_grad - total) * 0.25).astype(BF16)
            proj_grad_t[pl.ds(at, 16), cols] = dot(key, score_grad).astype(BF16)
            proj_grad_t[pl.ds(256 + at, 16), cols] = dot(query, score_grad, NT).astype(BF16)
            proj_grad_t[pl.ds(512 + at, 16), cols] = dot(grad, full.astype(BF16), NT).astype(BF16)
        return carry

    lax.fori_loop(0, HEADS, attend_back, 0, unroll=4)

    grad_t = proj_grad_t[...]
    first_t = first_in.T
    for part in range(3):
        qkv_grad = dot(first_t, grad_t[part * 256 : part * 256 + 256], NT)
        put(2 * part, slice(256, 384), qkv_grad[:, :128])
        put(2 * part + 1, slice(256, 384), qkv_grad[:, 128:])
    first_back = dot(grad_t, qkv_ref[...], ((0,), (1,)))
    grad = resid_grad + norm_back(normed_one, inverse_one, gain_first, first_back)
    grad = jnp.where(keep, grad, 0.0).astype(BF16)
    slot = iota((256, 256), 0)
    want = slot // 4 % 2 * 128 + slot // 8 * 4 + slot % 4
    grad_ref[...] = dot((iota((256, 256), 1) == want).astype(BF16), grad).astype(BF16)


def core_sum_kernel(mine_ref, other_ref, *outs):
    for slot, out_ref in enumerate(outs):
        total = mine_ref[slot].astype(F32) + other_ref[slot].astype(F32)
        out_ref[...] = total.astype(BF16)


def x_sum_kernel(own_ref, one_ref, two_ref, three_ref, grad_ref, out_ref):
    total = own_ref[...].astype(F32) + one_ref[...].astype(F32)
    total = total + two_ref[...].astype(F32) + three_ref[...].astype(F32)
    out_ref[:, :, 0:384] = total.astype(BF16).reshape(32, 8, 384)
    out_ref[:, :, 384:640] = grad_ref[...].reshape(32, 8, 256)


def yz_sum_kernel(joint_ref, valid_ref, total_ref, out_ref):
    total = jnp.sum(joint_ref[:, :, 0:384].astype(F32), axis=0).astype(BF16)
    total_ref[...] = jnp.broadcast_to(total[None], total_ref.shape)
    valid = valid_ref[...]
    for group in range(2):
        match = slot_matrix(valid, group, 8).astype(BF16)
        back = joint_ref[group * 16 : group * 16 + 16, :, 384:640].reshape(128, 256)
        out_ref[pl.ds(group * 256, 256), :] = dot(match, back, TN).astype(BF16)


def spread_kernel(mine_ref, other_ref, qkv_ref, out_ref, up_ref, down_ref):
    core = lax.axis_index("c")
    for group in range(8):
        for lane in range(4):
            rows = slice(lane * 64, lane * 64 + 64)
            near = mine_ref[lane, group // 2].astype(F32)
            far = other_ref[lane, group // 2].astype(F32)
            piece = jnp.where(core == group % 2, near, far)
            if group < 4:
                up_ref[rows, pl.ds(group * 256, 256)] = piece[:, :256]
            else:
                down_ref[pl.ds((group - 4) * 256 + lane * 64, 64), :] = piece[:, :256]
            if group < 6:
                qkv_ref[rows, pl.ds(group * 128, 128)] = piece[:, 256:]
            else:
                out_ref[rows, pl.ds((group - 6) * 128, 128)] = piece[:, 256:]


def run(kernel, out_shape, *args, scratch=(), held=()):
    specs = [
        pl.BlockSpec(memory_space=pltpu.HBM if at in held else pltpu.VMEM)
        for at in range(len(args))
    ]
    return pl.pallas_call(
        kernel,
        out_shape=out_shape,
        in_specs=specs,
        scratch_shapes=list(scratch),
        compiler_params=pltpu.CompilerParams(vmem_limit_bytes=VMEM_LIMIT),
    )(*args)


def shift(array, axis, size, by):
    return lax.ppermute(array, axis, [(at, (at + by) % size) for at in range(size)])


def per_device(
    features,
    cotangent,
    valid_dates,
    gain_first,
    qkv_weight,
    out_weight,
    gain_second,
    up_weight,
    down_weight,
):
    shape = jax.ShapeDtypeStruct
    width = features.shape[-1]
    scale = float(256 * 2 * 256) ** (-0.5)
    dates = ("y", "z")
    with jax.named_scope("compact"):
        send = run(
            compact_kernel,
            shape((512, width), BF16),
            features.reshape(512, width),
            cotangent.reshape(512, width),
            valid_dates,
            held=(0, 1),
            scratch=(
                pltpu.VMEM((512, width), BF16),
                pltpu.VMEM((512, width), BF16),
                pltpu.SemaphoreType.DMA((2, 2)),
            ),
        )
    with jax.named_scope("to_owner"):
        recv = lax.all_to_all(
            send.reshape(32, 16, width), dates, split_axis=0, concat_axis=0, tiled=True
        )
    half = shape((4, 256, 384), BF16)
    piece = shape((256, 384), BF16)
    with jax.named_scope("layer"):
        grad, mine, theirs = run(
            functools.partial(layer_kernel, scale),
            (shape((256, width), BF16), half, half),
            recv.reshape(512, width),
            gain_first.reshape(1, width),
            qkv_weight,
            out_weight,
            gain_second.reshape(1, width),
            up_weight,
            down_weight,
            held=range(1, 7),
            scratch=(
                pltpu.VMEM((1, width), F32),
                pltpu.VMEM((256, 768), BF16),
                pltpu.VMEM((256, 256), BF16),
                pltpu.VMEM((1, width), F32),
                pltpu.VMEM((256, 1024), BF16),
                pltpu.VMEM((1024, 256), BF16),
                pltpu.SemaphoreType.DMA((6,)),
                pltpu.VMEM((2, HEADS, 128, 128), F32),
                pltpu.VMEM((768, 256), BF16),
                pltpu.VMEM((256, 256), BF16),
                pltpu.VMEM((256, 256), BF16),
                pltpu.VMEM((768, 256), BF16),
            ),
        )
    with jax.named_scope("core_sum"):
        other = shift(theirs, "c", 2, 1)
        slots = run(core_sum_kernel, (piece,) * 4, mine, other)
    with jax.named_scope("x_sum"):
        got = [shift(slots[by], "x", 4, by) for by in (1, 3, 2)]
        joint = run(x_sum_kernel, shape((32, 8, 640), BF16), slots[0], *got, grad)
    with jax.named_scope("yz_sum"):
        joint = lax.all_to_all(joint, dates, split_axis=0, concat_axis=0, tiled=True)
        total, feature_grad = run(
            yz_sum_kernel,
            (shape((8, 8, 384), BF16), shape((512, width), BF16)),
            joint,
            valid_dates,
        )
    with jax.named_scope("z_gather"):
        part = lax.all_to_all(total, "z", split_axis=0, concat_axis=0, tiled=True)
    with jax.named_scope("yx_gather"):
        part = jnp.broadcast_to(part.reshape(1, 64, 384), (16, 64, 384))
        mine = lax.all_to_all(part, ("y", "x"), split_axis=0, concat_axis=0, tiled=True)
    with jax.named_scope("core_gather"):
        other = shift(mine, "c", 2, 1)
    with jax.named_scope("spread"):
        outs = run(
            spread_kernel,
            (
                shape((256, 768), F32),
                shape((256, 256), F32),
                shape((256, 1024), F32),
                shape((1024, 256), F32),
            ),
            mine.reshape(4, 4, 64, 384),
            other.reshape(4, 4, 64, 384),
        )
    return (feature_grad.reshape(features.shape), *outs)


def solution(mesh):
    fine = Mesh(mesh.devices.reshape(4, 8, 4, 2), ("y", "z", "x", "c"))
    dates, tiles = ("y", "z"), ("x", "c")
    in_specs = (
        P(tiles, None, dates, None),
        P(tiles, None, dates, None),
        P(tiles, dates),
        P(),
        P(),
        P(),
        P(),
        P(),
        P(),
    )
    out_specs = (P(tiles, None, dates, None), P(), P(), P(), P())
    return jax.shard_map(
        per_device, mesh=fine, in_specs=in_specs, out_specs=out_specs, check_vma=False
    )
```

```python
import functools

import jax
import jax.numpy as jnp
from jax import lax
from jax.experimental import pallas as pl
from jax.experimental.pallas import tpu as pltpu
from jax.sharding import Mesh
from jax.sharding import PartitionSpec as P

HEADS = 16
CAP = 4
EPS = 1e-05
GELU_C = 0.7978845608028654
GELU_A = 0.044715
ABSENT = 2.0**100

F32 = jnp.float32
BF16 = jnp.bfloat16
VMEM_LIMIT = 48 * 1024 * 1024


def iota(shape, axis):
    return lax.broadcasted_iota(jnp.int32, shape, axis)


def dot(left, right, dims=((1,), (0,))):
    return lax.dot_general(left, right, (dims, ((), ())), preferred_element_type=F32)


TN = ((0,), (0,))
NT = ((1,), (1,))


def slot_matrix(valid, group, rows_per_block):
    date = iota((8, 256), 1) % 8
    day = iota((8, 256), 0)
    held = valid[group * 16 : group * 16 + 16, :].astype(F32)
    keep_all = dot(held, (day == date).astype(F32))
    rank_all = dot(held, (day < date).astype(F32))
    own = iota((16, 256), 0) == iota((16, 256), 1) // 16
    keep = jnp.sum(jnp.where(own, keep_all, 0.0), axis=0, keepdims=True)
    rank = jnp.sum(jnp.where(own, rank_all, 0.0), axis=0, keepdims=True)
    shape = (16 * rows_per_block, 256)
    row, col = iota(shape, 0), iota(shape, 1)
    match = (
        (row // rows_per_block == col // 16)
        & ((row // 4) % 2 == (col // 8) % 2)
        & (rank == (row % 4).astype(F32))
        & (keep > 0.5)
    )
    return match.astype(F32)


def compact_kernel(feat_ref, cot_ref, valid_ref, send_ref):
    valid = valid_ref[...]
    for group in range(2):
        match = slot_matrix(valid, group, 16)
        is_feat = (iota((256, 1), 0) // 8) % 2 == 0
        pick_feat = jnp.where(is_feat, match, 0.0).astype(BF16)
        pick_cot = jnp.where(is_feat, 0.0, match).astype(BF16)
        rows = pl.ds(group * 256, 256)
        got = dot(pick_feat, feat_ref[rows, :]) + dot(pick_cot, cot_ref[rows, :])
        filled = jnp.sum(match, axis=1, keepdims=True) > 0.5
        got = jnp.where(is_feat & jnp.logical_not(filled), ABSENT, got)
        send_ref[rows, :] = got.astype(BF16)


def row_mean(values):
    return jnp.sum(values, axis=-1, keepdims=True) * (1.0 / values.shape[-1])


def norm_rows(hidden):
    centre = hidden - row_mean(hidden)
    inverse = lax.rsqrt(row_mean(centre * centre) + EPS)
    return centre * inverse, inverse


def norm_back(normed, inverse, gain, upstream):
    scaled = upstream * gain
    return inverse * (scaled - row_mean(scaled) - normed * row_mean(scaled * normed))


def layer_kernel(
    scale,
    recv_ref,
    gain_first_ref,
    qkv_ref,
    out_w_ref,
    gain_second_ref,
    up_ref,
    down_ref,
    grad_ref,
    terms_ref,
    probs,
    proj_t,
    att_t,
    att_grad_t,
    proj_grad_t,
):
    core = lax.axis_index("c")
    place = lax.axis_index("x")

    def put(group, columns, value):
        slot = lax.rem(group // 2 - place + 4, 4)
        terms_ref[(group % 2) ^ core, slot, :, columns] = (value * scale).astype(BF16)

    token = iota((256, 512), 0)
    target = (token % 128) // 4 * 16 + token // 128 * 4 + token % 4
    source = iota((256, 512), 1)
    recv = recv_ref[...]
    inputs = dot((source == target).astype(BF16), recv)
    upstream = dot((source == target + 8).astype(BF16), recv).astype(BF16)
    keep = inputs[:, 0:1] < 0.5 * ABSENT
    inputs = jnp.where(keep, inputs, 0.0)
    gain_first = gain_first_ref[...]
    gain_second = gain_second_ref[...]

    normed_one, inverse_one = norm_rows(inputs)
    first_in = (normed_one * gain_first).astype(BF16)
    proj_t[...] = dot(qkv_ref[...], first_in, ((0,), (1,))).astype(BF16)

    def attend(head, carry):
        at = pl.multiple_of(head * 16, 16)
        for pix in range(2):
            cols = pl.ds(pix * 128, 128)
            query = proj_t[pl.ds(at, 16), cols]
            key = proj_t[pl.ds(256 + at, 16), cols]
            value = proj_t[pl.ds(512 + at, 16), cols]
            scores = dot(key, query, TN) * 0.25
            scores = jnp.where(keep[pix * 128 : pix * 128 + 128], scores, -1e30)
            powered = jnp.exp(scores - jnp.max(scores, axis=0, keepdims=True))
            full = powered * (1.0 / jnp.sum(powered, axis=0, keepdims=True))
            probs[pix, head] = full
            att_t[pl.ds(at, 16), cols] = dot(value, full.astype(BF16)).astype(BF16)
        return carry

    lax.fori_loop(0, HEADS, attend, 0, unroll=4)

    attended_t = att_t[...]
    out_w = out_w_ref[...]
    residual = inputs + dot(attended_t, out_w, TN)
    normed_two, inverse_two = norm_rows(residual)
    second_in = (normed_two * gain_second).astype(BF16)
    back = jnp.zeros((256, 256), F32)
    for part in range(4):
        cols = pl.ds(part * 256, 256)
        up_part = up_ref[:, cols]
        pre = dot(second_in, up_part)
        tangent = jnp.tanh(GELU_C * (pre + GELU_A * pre * pre * pre))
        activated = (0.5 * pre * (1.0 + tangent)).astype(BF16)
        slope = 0.5 * (1.0 + tangent) + 0.5 * pre * (1.0 - tangent * tangent) * GELU_C * (
            1.0 + 3.0 * GELU_A * pre * pre
        )
        put(4 + part, slice(0, 256), dot(activated, upstream, TN))
        hidden_grad = (dot(upstream, down_ref[cols, :], NT) * slope).astype(BF16)
        put(part, slice(0, 256), dot(second_in, hidden_grad, TN))
        back = back + dot(hidden_grad, up_part, NT)
    resid_grad = upstream.astype(F32) + norm_back(normed_two, inverse_two, gain_second, back)
    resid_half = resid_grad.astype(BF16)
    out_grad = dot(attended_t, resid_half)
    put(6, slice(256, 384), out_grad[:, :128])
    put(7, slice(256, 384), out_grad[:, 128:])
    att_grad_t[...] = dot(out_w, resid_half, NT).astype(BF16)

    def attend_back(head, carry):
        at = pl.multiple_of(head * 16, 16)
        for pix in range(2):
            cols = pl.ds(pix * 128, 128)
            query = proj_t[pl.ds(at, 16), cols]
            key = proj_t[pl.ds(256 + at, 16), cols]
            value = proj_t[pl.ds(512 + at, 16), cols]
            grad = att_grad_t[pl.ds(at, 16), cols]
            full = probs[pix, head]
            prob_grad = dot(value, grad, TN)
            total = jnp.sum(full * prob_grad, axis=0, keepdims=True)
            score_grad = (full * (prob_grad - total) * 0.25).astype(BF16)
            proj_grad_t[pl.ds(at, 16), cols] = dot(key, score_grad).astype(BF16)
            proj_grad_t[pl.ds(256 + at, 16), cols] = dot(query, score_grad, NT).astype(BF16)
            proj_grad_t[pl.ds(512 + at, 16), cols] = dot(grad, full.astype(BF16), NT).astype(BF16)
        return carry

    lax.fori_loop(0, HEADS, attend_back, 0, unroll=4)

    grad_t = proj_grad_t[...]
    first_t = first_in.T
    for part in range(3):
        qkv_grad = dot(first_t, grad_t[part * 256 : part * 256 + 256], NT)
        put(2 * part, slice(256, 384), qkv_grad[:, :128])
        put(2 * part + 1, slice(256, 384), qkv_grad[:, 128:])
    first_back = dot(grad_t, qkv_ref[...], ((0,), (1,)))
    grad = resid_grad + norm_back(normed_one, inverse_one, gain_first, first_back)
    grad = jnp.where(keep, grad, 0.0).astype(BF16)
    slot = iota((256, 256), 0)
    want = slot // 4 % 2 * 128 + slot // 8 * 4 + slot % 4
    grad_ref[...] = dot((iota((256, 256), 1) == want).astype(BF16), grad).astype(BF16)


def core_sum_kernel(terms_ref, other_ref, *outs):
    for slot, out_ref in enumerate(outs):
        total = terms_ref[0, slot].astype(F32) + other_ref[slot].astype(F32)
        out_ref[...] = total.astype(BF16)


def x_sum_kernel(own_ref, one_ref, two_ref, three_ref, grad_ref, out_ref):
    total = own_ref[...].astype(F32) + one_ref[...].astype(F32)
    total = total + two_ref[...].astype(F32) + three_ref[...].astype(F32)
    out_ref[:, :, 0:384] = total.astype(BF16).reshape(32, 8, 384)
    out_ref[:, :, 384:640] = grad_ref[...].reshape(32, 8, 256)


def yz_sum_kernel(joint_ref, valid_ref, total_ref, out_ref):
    total = jnp.sum(joint_ref[:, :, 0:384].astype(F32), axis=0).astype(BF16)
    total_ref[...] = jnp.broadcast_to(total[None], total_ref.shape)
    valid = valid_ref[...]
    for group in range(2):
        match = slot_matrix(valid, group, 8).astype(BF16)
        back = joint_ref[group * 16 : group * 16 + 16, :, 384:640].reshape(128, 256)
        out_ref[pl.ds(group * 256, 256), :] = dot(match, back, TN).astype(BF16)


def spread_kernel(mine_ref, other_ref, qkv_ref, out_ref, up_ref, down_ref):
    core = lax.axis_index("c")
    for group in range(8):
        for lane in range(4):
            rows = slice(lane * 64, lane * 64 + 64)
            near = mine_ref[lane, group // 2].astype(F32)
            far = other_ref[lane, group // 2].astype(F32)
            piece = jnp.where(core == group % 2, near, far)
            if group < 4:
                up_ref[rows, pl.ds(group * 256, 256)] = piece[:, :256]
            else:
                down_ref[pl.ds((group - 4) * 256 + lane * 64, 64), :] = piece[:, :256]
            if group < 6:
                qkv_ref[rows, pl.ds(group * 128, 128)] = piece[:, 256:]
            else:
                out_ref[rows, pl.ds((group - 6) * 128, 128)] = piece[:, 256:]


def run(kernel, out_shape, *args, scratch=()):
    return pl.pallas_call(
        kernel,
        out_shape=out_shape,
        scratch_shapes=list(scratch),
        compiler_params=pltpu.CompilerParams(vmem_limit_bytes=VMEM_LIMIT),
    )(*args)


def shift(array, axis, size, by):
    return lax.ppermute(array, axis, [(at, (at + by) % size) for at in range(size)])


def per_device(
    features,
    cotangent,
    valid_dates,
    gain_first,
    qkv_weight,
    out_weight,
    gain_second,
    up_weight,
    down_weight,
):
    shape = jax.ShapeDtypeStruct
    width = features.shape[-1]
    scale = float(256 * 2 * 256) ** (-0.5)
    dates = ("y", "z")
    with jax.named_scope("compact"):
        send = run(
            compact_kernel,
            shape((512, width), BF16),
            features.reshape(512, width),
            cotangent.reshape(512, width),
            valid_dates,
        )
    with jax.named_scope("to_owner"):
        recv = lax.all_to_all(
            send.reshape(32, 16, width), dates, split_axis=0, concat_axis=0, tiled=True
        )
    piece = shape((256, 384), BF16)
    with jax.named_scope("layer"):
        grad, terms = run(
            functools.partial(layer_kernel, scale),
            (shape((256, width), BF16), shape((2, 4, 256, 384), BF16)),
            recv.reshape(512, width),
            gain_first.reshape(1, width),
            qkv_weight,
            out_weight,
            gain_second.reshape(1, width),
            up_weight,
            down_weight,
            scratch=(
                pltpu.VMEM((2, HEADS, 128, 128), F32),
                pltpu.VMEM((768, 256), BF16),
                pltpu.VMEM((256, 256), BF16),
                pltpu.VMEM((256, 256), BF16),
                pltpu.VMEM((768, 256), BF16),
            ),
        )
    with jax.named_scope("core_sum"):
        other = shift(terms[1], "c", 2, 1)
        slots = run(core_sum_kernel, (piece,) * 4, terms, other)
    with jax.named_scope("x_sum"):
        got = [shift(slots[by], "x", 4, by) for by in (1, 3, 2)]
        joint = run(x_sum_kernel, shape((32, 8, 640), BF16), slots[0], *got, grad)
    with jax.named_scope("yz_sum"):
        joint = lax.all_to_all(joint, dates, split_axis=0, concat_axis=0, tiled=True)
        total, feature_grad = run(
            yz_sum_kernel,
            (shape((8, 8, 384), BF16), shape((512, width), BF16)),
            joint,
            valid_dates,
        )
    with jax.named_scope("z_gather"):
        part = lax.all_to_all(total, "z", split_axis=0, concat_axis=0, tiled=True)
    with jax.named_scope("yx_gather"):
        part = jnp.broadcast_to(part.reshape(1, 64, 384), (16, 64, 384))
        mine = lax.all_to_all(part, ("y", "x"), split_axis=0, concat_axis=0, tiled=True)
    with jax.named_scope("core_gather"):
        other = shift(mine, "c", 2, 1)
    with jax.named_scope("spread"):
        outs = run(
            spread_kernel,
            (
                shape((256, 768), F32),
                shape((256, 256), F32),
                shape((256, 1024), F32),
                shape((1024, 256), F32),
            ),
            mine.reshape(4, 4, 64, 384),
            other.reshape(4, 4, 64, 384),
        )
    return (feature_grad.reshape(features.shape), *outs)


def solution(mesh):
    fine = Mesh(mesh.devices.reshape(4, 8, 4, 2), ("y", "z", "x", "c"))
    dates, tiles = ("y", "z"), ("x", "c")
    in_specs = (
        P(tiles, None, dates, None),
        P(tiles, None, dates, None),
        P(tiles, dates),
        P(),
        P(),
        P(),
        P(),
        P(),
        P(),
    )
    out_specs = (P(tiles, None, dates, None), P(), P(), P(), P())
    return jax.shard_map(
        per_device, mesh=fine, in_specs=in_specs, out_specs=out_specs, check_vma=False
    )
```

```python
import functools

import jax
import jax.numpy as jnp
from jax import lax
from jax.experimental import pallas as pl
from jax.experimental.pallas import tpu as pltpu
from jax.sharding import Mesh
from jax.sharding import PartitionSpec as P

HEADS = 16
BATCH = 16
CAP = 4
EPS = 1e-05
GELU_C = 0.7978845608028654
GELU_A = 0.044715
ABSENT = 2.0**100

F32 = jnp.float32
BF16 = jnp.bfloat16
VMEM_LIMIT = 48 * 1024 * 1024


def iota(shape, axis):
    return lax.broadcasted_iota(jnp.int32, shape, axis)


def dot(left, right, dims=((1,), (0,))):
    return lax.dot_general(left, right, (dims, ((), ())), preferred_element_type=F32)


TN = ((0,), (0,))
NT = ((1,), (1,))


def slot_matrix(valid, group, rows_per_block):
    date = iota((8, 256), 1) % 8
    day = iota((8, 256), 0)
    held = valid[group * 16 : group * 16 + 16, :].astype(F32)
    keep_all = dot(held, (day == date).astype(F32))
    rank_all = dot(held, (day < date).astype(F32))
    own = iota((16, 256), 0) == iota((16, 256), 1) // 16
    keep = jnp.sum(jnp.where(own, keep_all, 0.0), axis=0, keepdims=True)
    rank = jnp.sum(jnp.where(own, rank_all, 0.0), axis=0, keepdims=True)
    shape = (16 * rows_per_block, 256)
    row, col = iota(shape, 0), iota(shape, 1)
    match = (
        (row // rows_per_block == col // 16)
        & ((row // 4) % 2 == (col // 8) % 2)
        & (rank == (row % 4).astype(F32))
        & (keep > 0.5)
    )
    return match.astype(F32)


def compact_kernel(feat_ref, cot_ref, valid_ref, send_ref):
    valid = valid_ref[...]
    for group in range(2):
        match = slot_matrix(valid, group, 16)
        is_feat = (iota((256, 1), 0) // 8) % 2 == 0
        pick_feat = jnp.where(is_feat, match, 0.0).astype(BF16)
        pick_cot = jnp.where(is_feat, 0.0, match).astype(BF16)
        rows = pl.ds(group * 256, 256)
        got = dot(pick_feat, feat_ref[rows, :]) + dot(pick_cot, cot_ref[rows, :])
        filled = jnp.sum(match, axis=1, keepdims=True) > 0.5
        got = jnp.where(is_feat & jnp.logical_not(filled), ABSENT, got)
        send_ref[rows, :] = got.astype(BF16)


def row_mean(values):
    return jnp.sum(values, axis=-1, keepdims=True) * (1.0 / values.shape[-1])


def norm_rows(hidden):
    centre = hidden - row_mean(hidden)
    inverse = lax.rsqrt(row_mean(centre * centre) + EPS)
    return centre * inverse, inverse


def norm_back(normed, inverse, gain, upstream):
    scaled = upstream * gain
    return inverse * (scaled - row_mean(scaled) - normed * row_mean(scaled * normed))


def layer_kernel(
    scale,
    recv_ref,
    gain_first_ref,
    qkv_ref,
    out_w_ref,
    gain_second_ref,
    up_ref,
    down_ref,
    grad_ref,
    terms_ref,
    probs,
    proj_t,
    att_t,
    att_grad_t,
    proj_grad_t,
):
    core = lax.axis_index("c")
    place = lax.axis_index("x")

    def put(group, columns, value):
        slot = lax.rem(group // 2 - place + 4, 4)
        terms_ref[(group % 2) ^ core, slot, :, columns] = (value * scale).astype(BF16)

    token = iota((256, 512), 0)
    target = (token % 128) // 4 * 16 + token // 128 * 4 + token % 4
    source = iota((256, 512), 1)
    recv = recv_ref[...]
    inputs = dot((source == target).astype(BF16), recv)
    upstream = dot((source == target + 8).astype(BF16), recv).astype(BF16)
    keep = inputs[:, 0:1] < 0.5 * ABSENT
    inputs = jnp.where(keep, inputs, 0.0)
    gain_first = gain_first_ref[...]
    gain_second = gain_second_ref[...]

    normed_one, inverse_one = norm_rows(inputs)
    first_in = (normed_one * gain_first).astype(BF16)
    proj_t[...] = dot(qkv_ref[...], first_in, ((0,), (1,))).astype(BF16)

    def attend(batch, carry):
        units = [(pix, batch * BATCH + step) for step in range(BATCH) for pix in range(2)]
        scores, full = [], []
        for pix, head in units:
            at = pl.multiple_of(head * 16, 16)
            cols = pl.ds(pix * 128, 128)
            query = proj_t[pl.ds(at, 16), cols]
            key = proj_t[pl.ds(256 + at, 16), cols]
            scores.append(dot(key, query, TN))
        for (pix, head), score in zip(units, scores):
            score = jnp.where(keep[pix * 128 : pix * 128 + 128], score * 0.25, -1e30)
            powered = jnp.exp(score - jnp.max(score, axis=0, keepdims=True))
            full.append(powered * (1.0 / jnp.sum(powered, axis=0, keepdims=True)))
        for (pix, head), prob in zip(units, full):
            probs[pix, head] = prob
            at = pl.multiple_of(head * 16, 16)
            cols = pl.ds(pix * 128, 128)
            value = proj_t[pl.ds(512 + at, 16), cols]
            att_t[pl.ds(at, 16), cols] = dot(value, prob.astype(BF16)).astype(BF16)
        return carry

    lax.fori_loop(0, HEADS // BATCH, attend, 0)

    attended_t = att_t[...]
    out_w = out_w_ref[...]
    residual = inputs + dot(attended_t, out_w, TN)
    normed_two, inverse_two = norm_rows(residual)
    second_in = (normed_two * gain_second).astype(BF16)
    back = jnp.zeros((256, 256), F32)
    for part in range(4):
        cols = pl.ds(part * 256, 256)
        up_part = up_ref[:, cols]
        pre = dot(second_in, up_part)
        tangent = jnp.tanh(GELU_C * (pre + GELU_A * pre * pre * pre))
        activated = (0.5 * pre * (1.0 + tangent)).astype(BF16)
        slope = 0.5 * (1.0 + tangent) + 0.5 * pre * (1.0 - tangent * tangent) * GELU_C * (
            1.0 + 3.0 * GELU_A * pre * pre
        )
        put(4 + part, slice(0, 256), dot(activated, upstream, TN))
        hidden_grad = (dot(upstream, down_ref[cols, :], NT) * slope).astype(BF16)
        put(part, slice(0, 256), dot(second_in, hidden_grad, TN))
        back = back + dot(hidden_grad, up_part, NT)
    resid_grad = upstream.astype(F32) + norm_back(normed_two, inverse_two, gain_second, back)
    resid_half = resid_grad.astype(BF16)
    out_grad = dot(attended_t, resid_half)
    put(6, slice(256, 384), out_grad[:, :128])
    put(7, slice(256, 384), out_grad[:, 128:])
    att_grad_t[...] = dot(out_w, resid_half, NT).astype(BF16)

    def attend_back(batch, carry):
        units = [(pix, batch * BATCH + step) for step in range(BATCH) for pix in range(2)]
        prob_grads, score_grads, outs = [], [], []
        for pix, head in units:
            at = pl.multiple_of(head * 16, 16)
            cols = pl.ds(pix * 128, 128)
            value = proj_t[pl.ds(512 + at, 16), cols]
            prob_grads.append(dot(value, att_grad_t[pl.ds(at, 16), cols], TN))
        for (pix, head), prob_grad in zip(units, prob_grads):
            full = probs[pix, head]
            total = jnp.sum(full * prob_grad, axis=0, keepdims=True)
            score_grads.append((full * (prob_grad - total) * 0.25).astype(BF16))
        for (pix, head), score_grad in zip(units, score_grads):
            at = pl.multiple_of(head * 16, 16)
            cols = pl.ds(pix * 128, 128)
            query = proj_t[pl.ds(at, 16), cols]
            key = proj_t[pl.ds(256 + at, 16), cols]
            grad = att_grad_t[pl.ds(at, 16), cols]
            outs.append(
                (
                    dot(key, score_grad),
                    dot(score_grad, query, NT),
                    dot(probs[pix, head].astype(BF16), grad, NT),
                )
            )
        for (pix, head), got in zip(units, outs):
            at = pl.multiple_of(head * 16, 16)
            cols = pl.ds(pix * 128, 128)
            proj_grad_t[pl.ds(at, 16), cols] = got[0].astype(BF16)
            proj_grad_t[pl.ds(256 + at, 16), cols] = got[1].T.astype(BF16)
            proj_grad_t[pl.ds(512 + at, 16), cols] = got[2].T.astype(BF16)
        return carry

    lax.fori_loop(0, HEADS // BATCH, attend_back, 0)

    grad_t = proj_grad_t[...]
    first_t = first_in.T
    for part in range(3):
        qkv_grad = dot(first_t, grad_t[part * 256 : part * 256 + 256], NT)
        put(2 * part, slice(256, 384), qkv_grad[:, :128])
        put(2 * part + 1, slice(256, 384), qkv_grad[:, 128:])
    first_back = dot(grad_t, qkv_ref[...], ((0,), (1,)))
    grad = resid_grad + norm_back(normed_one, inverse_one, gain_first, first_back)
    grad = jnp.where(keep, grad, 0.0).astype(BF16)
    slot = iota((256, 256), 0)
    want = slot // 4 % 2 * 128 + slot // 8 * 4 + slot % 4
    grad_ref[...] = dot((iota((256, 256), 1) == want).astype(BF16), grad).astype(BF16)


def core_sum_kernel(terms_ref, other_ref, *outs):
    for slot, out_ref in enumerate(outs):
        total = terms_ref[0, slot].astype(F32) + other_ref[slot].astype(F32)
        out_ref[...] = total.astype(BF16)


def x_sum_kernel(own_ref, one_ref, two_ref, three_ref, grad_ref, out_ref):
    total = own_ref[...].astype(F32) + one_ref[...].astype(F32)
    total = total + two_ref[...].astype(F32) + three_ref[...].astype(F32)
    out_ref[:, :, 0:384] = total.astype(BF16).reshape(32, 8, 384)
    out_ref[:, :, 384:640] = grad_ref[...].reshape(32, 8, 256)


def yz_sum_kernel(joint_ref, valid_ref, total_ref, out_ref):
    total = jnp.sum(joint_ref[:, :, 0:384].astype(F32), axis=0).astype(BF16)
    total_ref[...] = jnp.broadcast_to(total[None], total_ref.shape)
    valid = valid_ref[...]
    for group in range(2):
        match = slot_matrix(valid, group, 8).astype(BF16)
        back = joint_ref[group * 16 : group * 16 + 16, :, 384:640].reshape(128, 256)
        out_ref[pl.ds(group * 256, 256), :] = dot(match, back, TN).astype(BF16)


def spread_kernel(mine_ref, other_ref, qkv_ref, out_ref, up_ref, down_ref):
    core = lax.axis_index("c")
    for group in range(8):
        for lane in range(4):
            rows = slice(lane * 64, lane * 64 + 64)
            near = mine_ref[lane, group // 2].astype(F32)
            far = other_ref[lane, group // 2].astype(F32)
            piece = jnp.where(core == group % 2, near, far)
            if group < 4:
                up_ref[rows, pl.ds(group * 256, 256)] = piece[:, :256]
            else:
                down_ref[pl.ds((group - 4) * 256 + lane * 64, 64), :] = piece[:, :256]
            if group < 6:
                qkv_ref[rows, pl.ds(group * 128, 128)] = piece[:, 256:]
            else:
                out_ref[rows, pl.ds((group - 6) * 128, 128)] = piece[:, 256:]


def run(kernel, out_shape, *args, scratch=()):
    return pl.pallas_call(
        kernel,
        out_shape=out_shape,
        scratch_shapes=list(scratch),
        compiler_params=pltpu.CompilerParams(vmem_limit_bytes=VMEM_LIMIT),
    )(*args)


def shift(array, axis, size, by):
    return lax.ppermute(array, axis, [(at, (at + by) % size) for at in range(size)])


def per_device(
    features,
    cotangent,
    valid_dates,
    gain_first,
    qkv_weight,
    out_weight,
    gain_second,
    up_weight,
    down_weight,
):
    shape = jax.ShapeDtypeStruct
    width = features.shape[-1]
    scale = float(256 * 2 * 256) ** (-0.5)
    dates = ("y", "z")
    with jax.named_scope("compact"):
        send = run(
            compact_kernel,
            shape((512, width), BF16),
            features.reshape(512, width),
            cotangent.reshape(512, width),
            valid_dates,
        )
    with jax.named_scope("to_owner"):
        recv = lax.all_to_all(
            send.reshape(32, 16, width), dates, split_axis=0, concat_axis=0, tiled=True
        )
    piece = shape((256, 384), BF16)
    with jax.named_scope("layer"):
        grad, terms = run(
            functools.partial(layer_kernel, scale),
            (shape((256, width), BF16), shape((2, 4, 256, 384), BF16)),
            recv.reshape(512, width),
            gain_first.reshape(1, width),
            qkv_weight,
            out_weight,
            gain_second.reshape(1, width),
            up_weight,
            down_weight,
            scratch=(
                pltpu.VMEM((2, HEADS, 128, 128), F32),
                pltpu.VMEM((768, 256), BF16),
                pltpu.VMEM((256, 256), BF16),
                pltpu.VMEM((256, 256), BF16),
                pltpu.VMEM((768, 256), BF16),
            ),
        )
    with jax.named_scope("core_sum"):
        other = shift(terms[1], "c", 2, 1)
        slots = run(core_sum_kernel, (piece,) * 4, terms, other)
    with jax.named_scope("x_sum"):
        got = [shift(slots[by], "x", 4, by) for by in (1, 3, 2)]
        joint = run(x_sum_kernel, shape((32, 8, 640), BF16), slots[0], *got, grad)
    with jax.named_scope("yz_sum"):
        joint = lax.all_to_all(joint, dates, split_axis=0, concat_axis=0, tiled=True)
        total, feature_grad = run(
            yz_sum_kernel,
            (shape((8, 8, 384), BF16), shape((512, width), BF16)),
            joint,
            valid_dates,
        )
    with jax.named_scope("z_gather"):
        part = lax.all_to_all(total, "z", split_axis=0, concat_axis=0, tiled=True)
    with jax.named_scope("yx_gather"):
        part = jnp.broadcast_to(part.reshape(1, 64, 384), (16, 64, 384))
        mine = lax.all_to_all(part, ("y", "x"), split_axis=0, concat_axis=0, tiled=True)
    with jax.named_scope("core_gather"):
        other = shift(mine, "c", 2, 1)
    with jax.named_scope("spread"):
        outs = run(
            spread_kernel,
            (
                shape((256, 768), F32),
                shape((256, 256), F32),
                shape((256, 1024), F32),
                shape((1024, 256), F32),
            ),
            mine.reshape(4, 4, 64, 384),
            other.reshape(4, 4, 64, 384),
        )
    return (feature_grad.reshape(features.shape), *outs)


def solution(mesh):
    fine = Mesh(mesh.devices.reshape(4, 8, 4, 2), ("y", "z", "x", "c"))
    dates, tiles = ("y", "z"), ("x", "c")
    in_specs = (
        P(tiles, None, dates, None),
        P(tiles, None, dates, None),
        P(tiles, dates),
        P(),
        P(),
        P(),
        P(),
        P(),
        P(),
    )
    out_specs = (P(tiles, None, dates, None), P(), P(), P(), P())
    return jax.shard_map(
        per_device, mesh=fine, in_specs=in_specs, out_specs=out_specs, check_vma=False
    )
```

```python
import functools

import jax
import jax.numpy as jnp
from jax import lax
from jax.experimental import pallas as pl
from jax.experimental.pallas import tpu as pltpu
from jax.sharding import Mesh
from jax.sharding import PartitionSpec as P

HEADS = 16
BATCH = 16
CAP = 4
EPS = 1e-05
GELU_C = 0.7978845608028654
GELU_A = 0.044715
ABSENT = 2.0**100

F32 = jnp.float32
BF16 = jnp.bfloat16
VMEM_LIMIT = 48 * 1024 * 1024


def iota(shape, axis):
    return lax.broadcasted_iota(jnp.int32, shape, axis)


def dot(left, right, dims=((1,), (0,))):
    return lax.dot_general(left, right, (dims, ((), ())), preferred_element_type=F32)


TN = ((0,), (0,))
NT = ((1,), (1,))


def slot_matrix(valid, group, rows_per_block):
    date = iota((8, 256), 1) % 8
    day = iota((8, 256), 0)
    held = valid.astype(F32)
    keep_all = dot(held, (day == date).astype(F32), TN)
    rank_all = dot(held, (day < date).astype(F32), TN)
    own = iota((32, 256), 0) == iota((32, 256), 1) // 16 + group * 16
    keep = jnp.sum(jnp.where(own, keep_all, 0.0), axis=0, keepdims=True)
    rank = jnp.sum(jnp.where(own, rank_all, 0.0), axis=0, keepdims=True)
    shape = (16 * rows_per_block, 256)
    row, col = iota(shape, 0), iota(shape, 1)
    match = (
        (row // rows_per_block == col // 16)
        & ((row // 4) % 2 == (col // 8) % 2)
        & (rank == (row % 4).astype(F32))
        & (keep > 0.5)
    )
    return match.astype(F32)


def compact_kernel(feat_hbm, cot_hbm, valid_hbm, send_ref, feat, cot, valid_ref, arrived):
    copies = [
        pltpu.make_async_copy(valid_hbm, valid_ref, arrived.at[0]),
        pltpu.make_async_copy(feat_hbm, feat, arrived.at[1]),
        pltpu.make_async_copy(cot_hbm, cot, arrived.at[2]),
    ]
    for copy in copies:
        copy.start()
    copies[0].wait()
    valid = valid_ref[...]
    is_feat = (iota((256, 1), 0) // 8) % 2 == 0
    picks = []
    for group in range(2):
        match = slot_matrix(valid, group, 16)
        pick_feat = jnp.where(is_feat, match, 0.0).astype(BF16)
        pick_cot = jnp.where(is_feat, 0.0, match).astype(BF16)
        filled = jnp.sum(match, axis=1, keepdims=True) > 0.5
        picks.append((pick_feat, pick_cot, is_feat & jnp.logical_not(filled)))
    copies[1].wait()
    copies[2].wait()
    for group, (pick_feat, pick_cot, absent) in enumerate(picks):
        rows = pl.ds(group * 256, 256)
        got = dot(pick_feat, feat[rows, :]) + dot(pick_cot, cot[rows, :])
        send_ref[rows, :] = jnp.where(absent, ABSENT, got).astype(BF16)


def row_mean(values):
    return jnp.sum(values, axis=-1, keepdims=True) * (1.0 / values.shape[-1])


def norm_rows(hidden):
    centre = hidden - row_mean(hidden)
    inverse = lax.rsqrt(row_mean(centre * centre) + EPS)
    return centre * inverse, inverse


def norm_back(normed, inverse, gain, upstream):
    scaled = upstream * gain
    return inverse * (scaled - row_mean(scaled) - normed * row_mean(scaled * normed))


def layer_kernel(
    scale,
    recv_ref,
    gain_first_hbm,
    qkv_hbm,
    out_w_hbm,
    gain_second_hbm,
    up_hbm,
    down_hbm,
    grad_ref,
    terms_ref,
    gain_first_ref,
    qkv_ref,
    out_w_ref,
    gain_second_ref,
    up_ref,
    down_ref,
    arrived,
    probs,
    proj_t,
    att_t,
    att_grad_t,
    proj_grad_t,
):
    pairs = (
        (qkv_hbm, qkv_ref),
        (gain_first_hbm, gain_first_ref),
        (out_w_hbm, out_w_ref),
        (gain_second_hbm, gain_second_ref),
        (up_hbm, up_ref),
        (down_hbm, down_ref),
    )
    copies = [
        pltpu.make_async_copy(held, ref, arrived.at[at]) for at, (held, ref) in enumerate(pairs)
    ]
    for copy in copies:
        copy.start()
    core = lax.axis_index("c")
    place = lax.axis_index("x")

    def put(group, columns, value):
        slot = lax.rem(group // 2 - place + 4, 4)
        terms_ref[(group % 2) ^ core, slot, :, columns] = (value * scale).astype(BF16)

    token = iota((256, 512), 0)
    target = (token % 128) // 4 * 16 + token // 128 * 4 + token % 4
    source = iota((256, 512), 1)
    recv = recv_ref[...]
    inputs = dot((source == target).astype(BF16), recv)
    upstream = dot((source == target + 8).astype(BF16), recv).astype(BF16)
    keep = inputs[:, 0:1] < 0.5 * ABSENT
    inputs = jnp.where(keep, inputs, 0.0)
    normed_one, inverse_one = norm_rows(inputs)
    copies[0].wait()
    copies[1].wait()
    gain_first = gain_first_ref[...]
    first_in = (normed_one * gain_first).astype(BF16)
    proj_t[...] = dot(qkv_ref[...], first_in, ((0,), (1,))).astype(BF16)

    def attend(batch, carry):
        units = [(pix, batch * BATCH + step) for step in range(BATCH) for pix in range(2)]
        scores, full = [], []
        for pix, head in units:
            at = pl.multiple_of(head * 16, 16)
            cols = pl.ds(pix * 128, 128)
            query = proj_t[pl.ds(at, 16), cols]
            key = proj_t[pl.ds(256 + at, 16), cols]
            scores.append(dot(key, query, TN))
        for (pix, head), score in zip(units, scores):
            score = jnp.where(keep[pix * 128 : pix * 128 + 128], score * 0.25, -1e30)
            powered = jnp.exp(score - jnp.max(score, axis=0, keepdims=True))
            full.append(powered * (1.0 / jnp.sum(powered, axis=0, keepdims=True)))
        for (pix, head), prob in zip(units, full):
            probs[pix, head] = prob
            at = pl.multiple_of(head * 16, 16)
            cols = pl.ds(pix * 128, 128)
            value = proj_t[pl.ds(512 + at, 16), cols]
            att_t[pl.ds(at, 16), cols] = dot(value, prob.astype(BF16)).astype(BF16)
        return carry

    lax.fori_loop(0, HEADS // BATCH, attend, 0)

    for copy in copies[2:]:
        copy.wait()
    gain_second = gain_second_ref[...]
    attended_t = att_t[...]
    out_w = out_w_ref[...]
    residual = inputs + dot(attended_t, out_w, TN)
    normed_two, inverse_two = norm_rows(residual)
    second_in = (normed_two * gain_second).astype(BF16)
    back = jnp.zeros((256, 256), F32)
    for part in range(4):
        cols = pl.ds(part * 256, 256)
        up_part = up_ref[:, cols]
        pre = dot(second_in, up_part)
        tangent = jnp.tanh(GELU_C * (pre + GELU_A * pre * pre * pre))
        activated = (0.5 * pre * (1.0 + tangent)).astype(BF16)
        slope = 0.5 * (1.0 + tangent) + 0.5 * pre * (1.0 - tangent * tangent) * GELU_C * (
            1.0 + 3.0 * GELU_A * pre * pre
        )
        put(4 + part, slice(0, 256), dot(activated, upstream, TN))
        hidden_grad = (dot(upstream, down_ref[cols, :], NT) * slope).astype(BF16)
        put(part, slice(0, 256), dot(second_in, hidden_grad, TN))
        back = back + dot(hidden_grad, up_part, NT)
    resid_grad = upstream.astype(F32) + norm_back(normed_two, inverse_two, gain_second, back)
    resid_half = resid_grad.astype(BF16)
    out_grad = dot(attended_t, resid_half)
    put(6, slice(256, 384), out_grad[:, :128])
    put(7, slice(256, 384), out_grad[:, 128:])
    att_grad_t[...] = dot(out_w, resid_half, NT).astype(BF16)

    def attend_back(batch, carry):
        units = [(pix, batch * BATCH + step) for step in range(BATCH) for pix in range(2)]
        prob_grads, score_grads, outs = [], [], []
        for pix, head in units:
            at = pl.multiple_of(head * 16, 16)
            cols = pl.ds(pix * 128, 128)
            value = proj_t[pl.ds(512 + at, 16), cols]
            prob_grads.append(dot(value, att_grad_t[pl.ds(at, 16), cols], TN))
        for (pix, head), prob_grad in zip(units, prob_grads):
            full = probs[pix, head]
            total = jnp.sum(full * prob_grad, axis=0, keepdims=True)
            score_grads.append((full * (prob_grad - total) * 0.25).astype(BF16))
        for (pix, head), score_grad in zip(units, score_grads):
            at = pl.multiple_of(head * 16, 16)
            cols = pl.ds(pix * 128, 128)
            query = proj_t[pl.ds(at, 16), cols]
            key = proj_t[pl.ds(256 + at, 16), cols]
            grad = att_grad_t[pl.ds(at, 16), cols]
            outs.append(
                (
                    dot(key, score_grad),
                    dot(score_grad, query, NT),
                    dot(probs[pix, head].astype(BF16), grad, NT),
                )
            )
        for (pix, head), got in zip(units, outs):
            at = pl.multiple_of(head * 16, 16)
            cols = pl.ds(pix * 128, 128)
            proj_grad_t[pl.ds(at, 16), cols] = got[0].astype(BF16)
            proj_grad_t[pl.ds(256 + at, 16), cols] = got[1].T.astype(BF16)
            proj_grad_t[pl.ds(512 + at, 16), cols] = got[2].T.astype(BF16)
        return carry

    lax.fori_loop(0, HEADS // BATCH, attend_back, 0)

    grad_t = proj_grad_t[...]
    first_t = first_in.T
    for part in range(3):
        qkv_grad = dot(first_t, grad_t[part * 256 : part * 256 + 256], NT)
        put(2 * part, slice(256, 384), qkv_grad[:, :128])
        put(2 * part + 1, slice(256, 384), qkv_grad[:, 128:])
    first_back = dot(grad_t, qkv_ref[...], ((0,), (1,)))
    grad = resid_grad + norm_back(normed_one, inverse_one, gain_first, first_back)
    grad = jnp.where(keep, grad, 0.0).astype(BF16)
    slot = iota((256, 256), 0)
    want = slot // 4 % 2 * 128 + slot // 8 * 4 + slot % 4
    grad_ref[...] = dot((iota((256, 256), 1) == want).astype(BF16), grad).astype(BF16)


def core_sum_kernel(terms_ref, other_ref, *outs):
    for slot, out_ref in enumerate(outs):
        total = terms_ref[0, slot].astype(F32) + other_ref[slot].astype(F32)
        out_ref[...] = total.astype(BF16)


def x_sum_kernel(own_ref, one_ref, two_ref, three_ref, grad_ref, out_ref):
    total = own_ref[...].astype(F32) + one_ref[...].astype(F32)
    total = total + two_ref[...].astype(F32) + three_ref[...].astype(F32)
    out_ref[:, :, 0:384] = total.astype(BF16).reshape(32, 8, 384)
    out_ref[:, :, 384:640] = grad_ref[...].reshape(32, 8, 256)


def yz_sum_kernel(joint_ref, valid_hbm, total_ref, out_ref, valid_ref, arrived):
    copy = pltpu.make_async_copy(valid_hbm, valid_ref, arrived)
    copy.start()
    total = jnp.sum(joint_ref[:, :, 0:384].astype(F32), axis=0).astype(BF16)
    total_ref[...] = jnp.broadcast_to(total[None], total_ref.shape)
    copy.wait()
    valid = valid_ref[...]
    for group in range(2):
        match = slot_matrix(valid, group, 8).astype(BF16)
        back = joint_ref[group * 16 : group * 16 + 16, :, 384:640].reshape(128, 256)
        out_ref[pl.ds(group * 256, 256), :] = dot(match, back, TN).astype(BF16)


def spread_kernel(flip, held_ref, *refs):
    qkv_hbm, out_hbm, up_hbm, down_hbm, wide, narrow, sent = refs[-7:]
    core = lax.axis_index("c") ^ flip
    copies = []
    for pair in range(4):
        group = 2 * pair + core
        for lane in range(4):
            rows = slice(lane * 64, lane * 64 + 64)
            piece = held_ref[lane, pair].astype(F32)
            wide[pair, rows, :] = piece[:, :256]
            narrow[pair, rows, :] = piece[:, 256:]
        if pair < 2:
            far = up_hbm.at[:, pl.ds(pl.multiple_of(group * 256, 256), 256)]
        else:
            far = down_hbm.at[pl.ds(pl.multiple_of((group - 4) * 256, 256), 256), :]
        if pair < 3:
            near = qkv_hbm.at[:, pl.ds(pl.multiple_of(group * 128, 128), 128)]
        else:
            near = out_hbm.at[:, pl.ds(pl.multiple_of((group - 6) * 128, 128), 128)]
        for source, target, at in ((wide, far, 0), (narrow, near, 1)):
            copy = pltpu.make_async_copy(source.at[pair], target, sent.at[pair, at])
            copy.start()
            copies.append(copy)
    for copy in copies:
        copy.wait()


def spread(flip, held, *outs):
    shape = jax.ShapeDtypeStruct
    kept = pl.BlockSpec(memory_space=pl.ANY)
    return pl.pallas_call(
        functools.partial(spread_kernel, flip),
        out_shape=(
            shape((256, 768), F32),
            shape((256, 256), F32),
            shape((256, 1024), F32),
            shape((1024, 256), F32),
        ),
        in_specs=[pl.BlockSpec(memory_space=pltpu.VMEM)] + [kept] * len(outs),
        out_specs=[kept] * 4,
        scratch_shapes=[
            pltpu.VMEM((4, 256, 256), F32),
            pltpu.VMEM((4, 256, 128), F32),
            pltpu.SemaphoreType.DMA((4, 2)),
        ],
        input_output_aliases={at + 1: at for at in range(len(outs))},
        compiler_params=pltpu.CompilerParams(vmem_limit_bytes=VMEM_LIMIT),
        cost_estimate=pl.CostEstimate(flops=0, bytes_accessed=3000000, transcendentals=0),
    )(held, *outs)


def stay(array):
    return pltpu.with_memory_space_constraint(array, pltpu.HBM)


def run(kernel, out_shape, *args, scratch=(), held=()):
    specs = [
        pl.BlockSpec(memory_space=pltpu.HBM if at in held else pltpu.VMEM)
        for at in range(len(args))
    ]
    args = [stay(array) if at in held else array for at, array in enumerate(args)]
    return pl.pallas_call(
        kernel,
        out_shape=out_shape,
        in_specs=specs,
        scratch_shapes=list(scratch),
        compiler_params=pltpu.CompilerParams(vmem_limit_bytes=VMEM_LIMIT),
    )(*args)


def shift(array, axis, size, by):
    return lax.ppermute(array, axis, [(at, (at + by) % size) for at in range(size)])


def per_device(
    features,
    cotangent,
    valid_dates,
    gain_first,
    qkv_weight,
    out_weight,
    gain_second,
    up_weight,
    down_weight,
):
    shape = jax.ShapeDtypeStruct
    width = features.shape[-1]
    scale = float(256 * 2 * 256) ** (-0.5)
    dates = ("y", "z")
    with jax.named_scope("compact"):
        send = run(
            compact_kernel,
            shape((512, width), BF16),
            features.reshape(512, width),
            cotangent.reshape(512, width),
            valid_dates.T,
            held=(0, 1, 2),
            scratch=(
                pltpu.VMEM((512, width), BF16),
                pltpu.VMEM((512, width), BF16),
                pltpu.VMEM((8, 32), jnp.int32),
                pltpu.SemaphoreType.DMA((3,)),
            ),
        )
    with jax.named_scope("to_owner"):
        recv = lax.all_to_all(
            send.reshape(32, 16, width), dates, split_axis=0, concat_axis=0, tiled=True
        )
    piece = shape((256, 384), BF16)
    with jax.named_scope("layer"):
        grad, terms = run(
            functools.partial(layer_kernel, scale),
            (shape((256, width), BF16), shape((2, 4, 256, 384), BF16)),
            recv.reshape(512, width),
            gain_first.reshape(1, width),
            qkv_weight,
            out_weight,
            gain_second.reshape(1, width),
            up_weight,
            down_weight,
            held=range(1, 7),
            scratch=(
                pltpu.VMEM((1, width), F32),
                pltpu.VMEM((256, 768), BF16),
                pltpu.VMEM((256, 256), BF16),
                pltpu.VMEM((1, width), F32),
                pltpu.VMEM((256, 1024), BF16),
                pltpu.VMEM((1024, 256), BF16),
                pltpu.SemaphoreType.DMA((6,)),
                pltpu.VMEM((2, HEADS, 128, 128), F32),
                pltpu.VMEM((768, 256), BF16),
                pltpu.VMEM((256, 256), BF16),
                pltpu.VMEM((256, 256), BF16),
                pltpu.VMEM((768, 256), BF16),
            ),
        )
    with jax.named_scope("core_sum"):
        other = shift(terms[1], "c", 2, 1)
        slots = run(core_sum_kernel, (piece,) * 4, terms, other)
    with jax.named_scope("x_sum"):
        got = [shift(slots[by], "x", 4, by) for by in (1, 3, 2)]
        joint = run(x_sum_kernel, shape((32, 8, 640), BF16), slots[0], *got, grad)
    with jax.named_scope("yz_sum"):
        joint = lax.all_to_all(joint, dates, split_axis=0, concat_axis=0, tiled=True)
        total, feature_grad = run(
            yz_sum_kernel,
            (shape((8, 8, 384), BF16), shape((512, width), BF16)),
            joint,
            valid_dates.T,
            held=(1,),
            scratch=(pltpu.VMEM((8, 32), jnp.int32), pltpu.SemaphoreType.DMA),
        )
    with jax.named_scope("z_gather"):
        part = lax.all_to_all(total, "z", split_axis=0, concat_axis=0, tiled=True)
    with jax.named_scope("yx_gather"):
        part = jnp.broadcast_to(part.reshape(1, 64, 384), (16, 64, 384))
        mine = lax.all_to_all(part, ("y", "x"), split_axis=0, concat_axis=0, tiled=True)
    with jax.named_scope("core_gather"):
        other = shift(mine, "c", 2, 1)
    with jax.named_scope("spread"):
        outs = spread(0, mine.reshape(4, 4, 64, 384))
        outs = spread(1, other.reshape(4, 4, 64, 384), *outs)
    return (feature_grad.reshape(features.shape), *outs)


def solution(mesh):
    fine = Mesh(mesh.devices.reshape(4, 8, 4, 2), ("y", "z", "x", "c"))
    dates, tiles = ("y", "z"), ("x", "c")
    in_specs = (
        P(tiles, None, dates, None),
        P(tiles, None, dates, None),
        P(tiles, dates),
        P(),
        P(),
        P(),
        P(),
        P(),
        P(),
    )
    out_specs = (P(tiles, None, dates, None), P(), P(), P(), P())
    return jax.shard_map(
        per_device, mesh=fine, in_specs=in_specs, out_specs=out_specs, check_vma=False
    )
```

```python
import functools

import jax
import jax.numpy as jnp
from jax import lax
from jax.experimental import pallas as pl
from jax.experimental.pallas import tpu as pltpu
from jax.sharding import Mesh
from jax.sharding import PartitionSpec as P

HEADS = 16
BATCH = 16
CAP = 4
EPS = 1e-05
GELU_C = 0.7978845608028654
GELU_A = 0.044715
ABSENT = 2.0**100

F32 = jnp.float32
BF16 = jnp.bfloat16
VMEM_LIMIT = 48 * 1024 * 1024


def iota(shape, axis):
    return lax.broadcasted_iota(jnp.int32, shape, axis)


def dot(left, right, dims=((1,), (0,))):
    return lax.dot_general(left, right, (dims, ((), ())), preferred_element_type=F32)


TN = ((0,), (0,))
NT = ((1,), (1,))


def slot_matrix(valid, group, rows_per_block):
    date = iota((8, 256), 1) % 8
    day = iota((8, 256), 0)
    held = valid.astype(F32)
    keep_all = dot(held, (day == date).astype(F32), TN)
    rank_all = dot(held, (day < date).astype(F32), TN)
    own = iota((32, 256), 0) == iota((32, 256), 1) // 16 + group * 16
    keep = jnp.sum(jnp.where(own, keep_all, 0.0), axis=0, keepdims=True)
    rank = jnp.sum(jnp.where(own, rank_all, 0.0), axis=0, keepdims=True)
    shape = (16 * rows_per_block, 256)
    row, col = iota(shape, 0), iota(shape, 1)
    match = (
        (row // rows_per_block == col // 16)
        & ((row // 4) % 2 == (col // 8) % 2)
        & (rank == (row % 4).astype(F32))
        & (keep > 0.5)
    )
    return match.astype(F32)


def compact_kernel(feat_hbm, cot_hbm, valid_hbm, send_ref, feat, cot, valid_ref, arrived):
    copies = [
        pltpu.make_async_copy(valid_hbm, valid_ref, arrived.at[0]),
        pltpu.make_async_copy(feat_hbm, feat, arrived.at[1]),
        pltpu.make_async_copy(cot_hbm, cot, arrived.at[2]),
    ]
    for copy in copies:
        copy.start()
    copies[0].wait()
    valid = valid_ref[...]
    is_feat = (iota((256, 1), 0) // 8) % 2 == 0
    picks = []
    for group in range(2):
        match = slot_matrix(valid, group, 16)
        pick_feat = jnp.where(is_feat, match, 0.0).astype(BF16)
        pick_cot = jnp.where(is_feat, 0.0, match).astype(BF16)
        filled = jnp.sum(match, axis=1, keepdims=True) > 0.5
        picks.append((pick_feat, pick_cot, is_feat & jnp.logical_not(filled)))
    copies[1].wait()
    copies[2].wait()
    for group, (pick_feat, pick_cot, absent) in enumerate(picks):
        rows = pl.ds(group * 256, 256)
        got = dot(pick_feat, feat[rows, :]) + dot(pick_cot, cot[rows, :])
        send_ref[rows, :] = jnp.where(absent, ABSENT, got).astype(BF16)


def row_mean(values):
    return jnp.sum(values, axis=-1, keepdims=True) * (1.0 / values.shape[-1])


def norm_rows(hidden):
    centre = hidden - row_mean(hidden)
    inverse = lax.rsqrt(row_mean(centre * centre) + EPS)
    return centre * inverse, inverse


def norm_back(normed, inverse, gain, upstream):
    scaled = upstream * gain
    return inverse * (scaled - row_mean(scaled) - normed * row_mean(scaled * normed))


def layer_kernel(
    scale,
    recv_ref,
    gain_first_hbm,
    qkv_hbm,
    out_w_hbm,
    gain_second_hbm,
    up_hbm,
    down_hbm,
    grad_ref,
    terms_ref,
    gain_first_ref,
    qkv_ref,
    out_w_ref,
    gain_second_ref,
    up_ref,
    down_ref,
    arrived,
    probs,
    proj_t,
    att_t,
    att_grad_t,
    proj_grad_t,
):
    pairs = (
        (qkv_hbm, qkv_ref),
        (gain_first_hbm, gain_first_ref),
        (out_w_hbm, out_w_ref),
        (gain_second_hbm, gain_second_ref),
        (up_hbm, up_ref),
        (down_hbm, down_ref),
    )
    copies = [
        pltpu.make_async_copy(held, ref, arrived.at[at]) for at, (held, ref) in enumerate(pairs)
    ]
    for copy in copies:
        copy.start()
    core = lax.axis_index("c")
    place = lax.axis_index("x")

    def put(group, columns, value):
        slot = lax.rem(group // 2 - place + 4, 4)
        terms_ref[(group % 2) ^ core, slot, :, columns] = (value * scale).astype(BF16)

    token = iota((256, 512), 0)
    target = (token % 128) // 4 * 16 + token // 128 * 4 + token % 4
    source = iota((256, 512), 1)
    recv = recv_ref[...]
    inputs = dot((source == target).astype(BF16), recv)
    upstream = dot((source == target + 8).astype(BF16), recv).astype(BF16)
    keep = inputs[:, 0:1] < 0.5 * ABSENT
    inputs = jnp.where(keep, inputs, 0.0)
    normed_one, inverse_one = norm_rows(inputs)
    copies[0].wait()
    copies[1].wait()
    gain_first = gain_first_ref[...]
    first_in = (normed_one * gain_first).astype(BF16)
    proj_t[...] = dot(qkv_ref[...], first_in, ((0,), (1,))).astype(BF16)

    def attend(batch, carry):
        units = [(pix, batch * BATCH + step) for step in range(BATCH) for pix in range(2)]
        scores, full = [], []
        for pix, head in units:
            at = pl.multiple_of(head * 16, 16)
            cols = pl.ds(pix * 128, 128)
            query = proj_t[pl.ds(at, 16), cols]
            key = proj_t[pl.ds(256 + at, 16), cols]
            scores.append(dot(key, query, TN))
        for (pix, head), score in zip(units, scores):
            score = jnp.where(keep[pix * 128 : pix * 128 + 128], score * 0.25, -1e30)
            powered = jnp.exp(score - jnp.max(score, axis=0, keepdims=True))
            full.append(powered * (1.0 / jnp.sum(powered, axis=0, keepdims=True)))
        for (pix, head), prob in zip(units, full):
            probs[pix, head] = prob
            at = pl.multiple_of(head * 16, 16)
            cols = pl.ds(pix * 128, 128)
            value = proj_t[pl.ds(512 + at, 16), cols]
            att_t[pl.ds(at, 16), cols] = dot(value, prob.astype(BF16)).astype(BF16)
        return carry

    lax.fori_loop(0, HEADS // BATCH, attend, 0)

    for copy in copies[2:]:
        copy.wait()
    gain_second = gain_second_ref[...]
    attended_t = att_t[...]
    out_w = out_w_ref[...]
    residual = inputs + dot(attended_t, out_w, TN)
    normed_two, inverse_two = norm_rows(residual)
    second_in = (normed_two * gain_second).astype(BF16)
    back = jnp.zeros((256, 256), F32)
    for part in range(4):
        cols = pl.ds(part * 256, 256)
        up_part = up_ref[:, cols]
        pre = dot(second_in, up_part)
        tangent = jnp.tanh(GELU_C * (pre + GELU_A * pre * pre * pre))
        activated = (0.5 * pre * (1.0 + tangent)).astype(BF16)
        slope = 0.5 * (1.0 + tangent) + 0.5 * pre * (1.0 - tangent * tangent) * GELU_C * (
            1.0 + 3.0 * GELU_A * pre * pre
        )
        put(4 + part, slice(0, 256), dot(activated, upstream, TN))
        hidden_grad = (dot(upstream, down_ref[cols, :], NT) * slope).astype(BF16)
        put(part, slice(0, 256), dot(second_in, hidden_grad, TN))
        back = back + dot(hidden_grad, up_part, NT)
    resid_grad = upstream.astype(F32) + norm_back(normed_two, inverse_two, gain_second, back)
    resid_half = resid_grad.astype(BF16)
    out_grad = dot(attended_t, resid_half)
    put(6, slice(256, 384), out_grad[:, :128])
    put(7, slice(256, 384), out_grad[:, 128:])
    att_grad_t[...] = dot(out_w, resid_half, NT).astype(BF16)

    def attend_back(batch, carry):
        units = [(pix, batch * BATCH + step) for step in range(BATCH) for pix in range(2)]
        prob_grads, score_grads, outs = [], [], []
        for pix, head in units:
            at = pl.multiple_of(head * 16, 16)
            cols = pl.ds(pix * 128, 128)
            value = proj_t[pl.ds(512 + at, 16), cols]
            prob_grads.append(dot(value, att_grad_t[pl.ds(at, 16), cols], TN))
        for (pix, head), prob_grad in zip(units, prob_grads):
            full = probs[pix, head]
            total = jnp.sum(full * prob_grad, axis=0, keepdims=True)
            score_grads.append((full * (prob_grad - total) * 0.25).astype(BF16))
        for (pix, head), score_grad in zip(units, score_grads):
            at = pl.multiple_of(head * 16, 16)
            cols = pl.ds(pix * 128, 128)
            query = proj_t[pl.ds(at, 16), cols]
            key = proj_t[pl.ds(256 + at, 16), cols]
            grad = att_grad_t[pl.ds(at, 16), cols]
            outs.append(
                (
                    dot(key, score_grad),
                    dot(score_grad, query, NT),
                    dot(probs[pix, head].astype(BF16), grad, NT),
                )
            )
        for (pix, head), got in zip(units, outs):
            at = pl.multiple_of(head * 16, 16)
            cols = pl.ds(pix * 128, 128)
            proj_grad_t[pl.ds(at, 16), cols] = got[0].astype(BF16)
            proj_grad_t[pl.ds(256 + at, 16), cols] = got[1].T.astype(BF16)
            proj_grad_t[pl.ds(512 + at, 16), cols] = got[2].T.astype(BF16)
        return carry

    lax.fori_loop(0, HEADS // BATCH, attend_back, 0)

    grad_t = proj_grad_t[...]
    first_t = first_in.T
    for part in range(3):
        qkv_grad = dot(first_t, grad_t[part * 256 : part * 256 + 256], NT)
        put(2 * part, slice(256, 384), qkv_grad[:, :128])
        put(2 * part + 1, slice(256, 384), qkv_grad[:, 128:])
    first_back = dot(grad_t, qkv_ref[...], ((0,), (1,)))
    grad = resid_grad + norm_back(normed_one, inverse_one, gain_first, first_back)
    grad = jnp.where(keep, grad, 0.0).astype(BF16)
    slot = iota((256, 256), 0)
    want = slot // 4 % 2 * 128 + slot // 8 * 4 + slot % 4
    grad_ref[...] = dot((iota((256, 256), 1) == want).astype(BF16), grad).astype(BF16)


def core_sum_kernel(terms_ref, other_ref, *outs):
    for slot, out_ref in enumerate(outs):
        total = terms_ref[0, slot].astype(F32) + other_ref[slot].astype(F32)
        out_ref[...] = total.astype(BF16)


def x_sum_kernel(own_ref, one_ref, two_ref, three_ref, grad_ref, out_ref):
    total = own_ref[...].astype(F32) + one_ref[...].astype(F32)
    total = total + two_ref[...].astype(F32) + three_ref[...].astype(F32)
    out_ref[:, :, 0:384] = total.astype(BF16).reshape(32, 8, 384)
    out_ref[:, :, 384:640] = grad_ref[...].reshape(32, 8, 256)


def yz_sum_kernel(joint_ref, total_ref):
    total = jnp.sum(joint_ref[:, :, 0:384].astype(F32), axis=0).astype(BF16)
    total_ref[...] = jnp.broadcast_to(total[None], total_ref.shape)


def expand_kernel(joint_ref, valid_hbm, out_ref, valid_ref, arrived):
    copy = pltpu.make_async_copy(valid_hbm, valid_ref, arrived)
    copy.start()
    copy.wait()
    valid = valid_ref[...]
    for group in range(2):
        match = slot_matrix(valid, group, 8).astype(BF16)
        back = joint_ref[group * 16 : group * 16 + 16, :, 384:640].reshape(128, 256)
        out_ref[pl.ds(group * 256, 256), :] = dot(match, back, TN).astype(BF16)


def spread_kernel(flip, held_ref, *refs):
    qkv_hbm, out_hbm, up_hbm, down_hbm, wide, narrow, sent = refs[-7:]
    core = lax.axis_index("c") ^ flip
    copies = []
    for pair in range(4):
        group = 2 * pair + core
        for lane in range(4):
            rows = slice(lane * 64, lane * 64 + 64)
            piece = held_ref[lane, pair].astype(F32)
            wide[pair, rows, :] = piece[:, :256]
            narrow[pair, rows, :] = piece[:, 256:]
        if pair < 2:
            far = up_hbm.at[:, pl.ds(pl.multiple_of(group * 256, 256), 256)]
        else:
            far = down_hbm.at[pl.ds(pl.multiple_of((group - 4) * 256, 256), 256), :]
        if pair < 3:
            near = qkv_hbm.at[:, pl.ds(pl.multiple_of(group * 128, 128), 128)]
        else:
            near = out_hbm.at[:, pl.ds(pl.multiple_of((group - 6) * 128, 128), 128)]
        for source, target, at in ((wide, far, 0), (narrow, near, 1)):
            copy = pltpu.make_async_copy(source.at[pair], target, sent.at[pair, at])
            copy.start()
            copies.append(copy)
    for copy in copies:
        copy.wait()


def spread(flip, held, *outs):
    shape = jax.ShapeDtypeStruct
    kept = pl.BlockSpec(memory_space=pl.ANY)
    return pl.pallas_call(
        functools.partial(spread_kernel, flip),
        out_shape=(
            shape((256, 768), F32),
            shape((256, 256), F32),
            shape((256, 1024), F32),
            shape((1024, 256), F32),
        ),
        in_specs=[pl.BlockSpec(memory_space=pltpu.VMEM)] + [kept] * len(outs),
        out_specs=[kept] * 4,
        scratch_shapes=[
            pltpu.VMEM((4, 256, 256), F32),
            pltpu.VMEM((4, 256, 128), F32),
            pltpu.SemaphoreType.DMA((4, 2)),
        ],
        input_output_aliases={at + 1: at for at in range(len(outs))},
        compiler_params=pltpu.CompilerParams(vmem_limit_bytes=VMEM_LIMIT),
        cost_estimate=pl.CostEstimate(flops=0, bytes_accessed=3000000, transcendentals=0),
    )(held, *outs)


def stay(array):
    return pltpu.with_memory_space_constraint(array, pltpu.HBM)


def run(kernel, out_shape, *args, scratch=(), held=(), cost=None):
    specs = [
        pl.BlockSpec(memory_space=pltpu.HBM if at in held else pltpu.VMEM)
        for at in range(len(args))
    ]
    args = [stay(array) if at in held else array for at, array in enumerate(args)]
    return pl.pallas_call(
        kernel,
        out_shape=out_shape,
        in_specs=specs,
        scratch_shapes=list(scratch),
        compiler_params=pltpu.CompilerParams(vmem_limit_bytes=VMEM_LIMIT),
        cost_estimate=cost
        and pl.CostEstimate(flops=0, bytes_accessed=cost, transcendentals=0),
    )(*args)


def shift(array, axis, size, by):
    return lax.ppermute(array, axis, [(at, (at + by) % size) for at in range(size)])


def per_device(
    features,
    cotangent,
    valid_dates,
    gain_first,
    qkv_weight,
    out_weight,
    gain_second,
    up_weight,
    down_weight,
):
    shape = jax.ShapeDtypeStruct
    width = features.shape[-1]
    scale = float(256 * 2 * 256) ** (-0.5)
    dates = ("y", "z")
    with jax.named_scope("compact"):
        send = run(
            compact_kernel,
            shape((512, width), BF16),
            features.reshape(512, width),
            cotangent.reshape(512, width),
            valid_dates.T,
            held=(0, 1, 2),
            scratch=(
                pltpu.VMEM((512, width), BF16),
                pltpu.VMEM((512, width), BF16),
                pltpu.VMEM((8, 32), jnp.int32),
                pltpu.SemaphoreType.DMA((3,)),
            ),
        )
    with jax.named_scope("to_owner"):
        recv = lax.all_to_all(
            send.reshape(32, 16, width), dates, split_axis=0, concat_axis=0, tiled=True
        )
    piece = shape((256, 384), BF16)
    with jax.named_scope("layer"):
        grad, terms = run(
            functools.partial(layer_kernel, scale),
            (shape((256, width), BF16), shape((2, 4, 256, 384), BF16)),
            recv.reshape(512, width),
            gain_first.reshape(1, width),
            qkv_weight,
            out_weight,
            gain_second.reshape(1, width),
            up_weight,
            down_weight,
            held=range(1, 7),
            scratch=(
                pltpu.VMEM((1, width), F32),
                pltpu.VMEM((256, 768), BF16),
                pltpu.VMEM((256, 256), BF16),
                pltpu.VMEM((1, width), F32),
                pltpu.VMEM((256, 1024), BF16),
                pltpu.VMEM((1024, 256), BF16),
                pltpu.SemaphoreType.DMA((6,)),
                pltpu.VMEM((2, HEADS, 128, 128), F32),
                pltpu.VMEM((768, 256), BF16),
                pltpu.VMEM((256, 256), BF16),
                pltpu.VMEM((256, 256), BF16),
                pltpu.VMEM((768, 256), BF16),
            ),
        )
    with jax.named_scope("core_sum"):
        other = shift(terms[1], "c", 2, 1)
        slots = run(core_sum_kernel, (piece,) * 4, terms, other)
    with jax.named_scope("x_sum"):
        got = [shift(slots[by], "x", 4, by) for by in (2, 1, 3)]
        joint = run(x_sum_kernel, shape((32, 8, 640), BF16), slots[0], *got, grad)
    with jax.named_scope("yz_sum"):
        joint = lax.all_to_all(joint, dates, split_axis=0, concat_axis=0, tiled=True)
        total = run(yz_sum_kernel, shape((8, 8, 384), BF16), joint)
    with jax.named_scope("z_gather"):
        part = lax.all_to_all(total, "z", split_axis=0, concat_axis=0, tiled=True)
    with jax.named_scope("yx_gather"):
        part = jnp.broadcast_to(part.reshape(1, 64, 384), (16, 64, 384))
        mine = lax.all_to_all(part, ("y", "x"), split_axis=0, concat_axis=0, tiled=True)
    with jax.named_scope("core_gather"):
        other = shift(mine, "c", 2, 1)
        joint, _ = lax.optimization_barrier((joint, mine))
    with jax.named_scope("expand"):
        feature_grad = run(
            expand_kernel,
            shape((512, width), BF16),
            joint,
            valid_dates.T,
            held=(1,),
            scratch=(pltpu.VMEM((8, 32), jnp.int32), pltpu.SemaphoreType.DMA),
            cost=1000000,
        )
    with jax.named_scope("spread"):
        outs = spread(0, mine.reshape(4, 4, 64, 384))
        outs = spread(1, other.reshape(4, 4, 64, 384), *outs)
    return (feature_grad.reshape(features.shape), *outs)


def solution(mesh):
    fine = Mesh(mesh.devices.reshape(4, 8, 4, 2), ("y", "z", "x", "c"))
    dates, tiles = ("y", "z"), ("x", "c")
    in_specs = (
        P(tiles, None, dates, None),
        P(tiles, None, dates, None),
        P(tiles, dates),
        P(),
        P(),
        P(),
        P(),
        P(),
        P(),
    )
    out_specs = (P(tiles, None, dates, None), P(), P(), P(), P())
    return jax.shard_map(
        per_device, mesh=fine, in_specs=in_specs, out_specs=out_specs, check_vma=False
    )
```

```python
import functools

import jax
import jax.numpy as jnp
from jax import lax
from jax.experimental import pallas as pl
from jax.experimental.pallas import tpu as pltpu
from jax.sharding import Mesh
from jax.sharding import PartitionSpec as P

HEADS = 16
BATCH = 16
CAP = 4
EPS = 1e-05
GELU_C = 0.7978845608028654
GELU_A = 0.044715
ABSENT = 2.0**100

F32 = jnp.float32
BF16 = jnp.bfloat16
VMEM_LIMIT = 48 * 1024 * 1024


def iota(shape, axis):
    return lax.broadcasted_iota(jnp.int32, shape, axis)


def dot(left, right, dims=((1,), (0,))):
    return lax.dot_general(left, right, (dims, ((), ())), preferred_element_type=F32)


TN = ((0,), (0,))
NT = ((1,), (1,))


def slot_matrix(valid, group):
    date = iota((8, 256), 1) % 8
    day = iota((8, 256), 0)
    held = valid.astype(F32)
    keep_all = dot(held, (day == date).astype(F32), TN)
    rank_all = dot(held, (day < date).astype(F32), TN)
    own = iota((32, 256), 0) == iota((32, 256), 1) // 16 + group * 16
    keep = jnp.sum(jnp.where(own, keep_all, 0.0), axis=0, keepdims=True)
    rank = jnp.sum(jnp.where(own, rank_all, 0.0), axis=0, keepdims=True)
    shape = (256, 256)
    row, col = iota(shape, 0), iota(shape, 1)
    match = (
        (row // 16 == col // 16)
        & ((row // 4) % 2 == (col // 8) % 2)
        & (rank == (row % 4).astype(F32))
        & (keep > 0.5)
    )
    return match.astype(F32)


def compact_kernel(feat_hbm, cot_hbm, valid_hbm, send_ref, match_ref, feat, cot, valid_ref, arrived):
    copies = [
        pltpu.make_async_copy(valid_hbm, valid_ref, arrived.at[0]),
        pltpu.make_async_copy(feat_hbm, feat, arrived.at[1]),
        pltpu.make_async_copy(cot_hbm, cot, arrived.at[2]),
    ]
    for copy in copies:
        copy.start()
    copies[0].wait()
    valid = valid_ref[...]
    is_feat = (iota((256, 1), 0) // 8) % 2 == 0
    picks = []
    for group in range(2):
        match = slot_matrix(valid, group)
        pick_feat = jnp.where(is_feat, match, 0.0).astype(BF16)
        pick_cot = jnp.where(is_feat, 0.0, match).astype(BF16)
        filled = jnp.sum(match, axis=1, keepdims=True) > 0.5
        match_ref[group] = match.reshape(16, 16, 256)[:, :8].reshape(128, 256).astype(BF16)
        picks.append((pick_feat, pick_cot, is_feat & jnp.logical_not(filled)))
    copies[1].wait()
    copies[2].wait()
    for group, (pick_feat, pick_cot, absent) in enumerate(picks):
        rows = pl.ds(group * 256, 256)
        got = dot(pick_feat, feat[rows, :]) + dot(pick_cot, cot[rows, :])
        send_ref[rows, :] = jnp.where(absent, ABSENT, got).astype(BF16)


def row_mean(values):
    return jnp.sum(values, axis=-1, keepdims=True) * (1.0 / values.shape[-1])


def norm_rows(hidden):
    centre = hidden - row_mean(hidden)
    inverse = lax.rsqrt(row_mean(centre * centre) + EPS)
    return centre * inverse, inverse


def norm_back(normed, inverse, gain, upstream):
    scaled = upstream * gain
    return inverse * (scaled - row_mean(scaled) - normed * row_mean(scaled * normed))


def layer_kernel(
    scale,
    recv_ref,
    gain_first_hbm,
    qkv_hbm,
    out_w_hbm,
    gain_second_hbm,
    up_hbm,
    down_hbm,
    grad_ref,
    *rest,
):
    (*sent_refs, gain_first_ref, qkv_ref, out_w_ref, gain_second_ref, up_ref, down_ref) = rest[:14]
    arrived, probs, proj_t, att_t, att_grad_t, proj_grad_t, terms_ref = rest[14:]
    pairs = (
        (qkv_hbm, qkv_ref),
        (gain_first_hbm, gain_first_ref),
        (out_w_hbm, out_w_ref),
        (gain_second_hbm, gain_second_ref),
        (up_hbm, up_ref),
        (down_hbm, down_ref),
    )
    copies = [
        pltpu.make_async_copy(held, ref, arrived.at[at]) for at, (held, ref) in enumerate(pairs)
    ]
    for copy in copies:
        copy.start()
    core = lax.axis_index("c")
    place = lax.axis_index("x")

    def put(group, columns, value):
        slot = lax.rem(group // 2 - place + 4, 4)
        terms_ref[(group % 2) ^ core, slot, :, columns] = (value * scale).astype(BF16)

    token = iota((256, 512), 0)
    target = (token % 128) // 4 * 16 + token // 128 * 4 + token % 4
    source = iota((256, 512), 1)
    recv = recv_ref[...]
    inputs = dot((source == target).astype(BF16), recv)
    upstream = dot((source == target + 8).astype(BF16), recv).astype(BF16)
    keep = inputs[:, 0:1] < 0.5 * ABSENT
    inputs = jnp.where(keep, inputs, 0.0)
    normed_one, inverse_one = norm_rows(inputs)
    copies[0].wait()
    copies[1].wait()
    gain_first = gain_first_ref[...]
    first_in = (normed_one * gain_first).astype(BF16)
    proj_t[...] = dot(qkv_ref[...], first_in, ((0,), (1,))).astype(BF16)

    def attend(batch, carry):
        units = [(pix, batch * BATCH + step) for step in range(BATCH) for pix in range(2)]
        scores, full = [], []
        for pix, head in units:
            at = pl.multiple_of(head * 16, 16)
            cols = pl.ds(pix * 128, 128)
            query = proj_t[pl.ds(at, 16), cols]
            key = proj_t[pl.ds(256 + at, 16), cols]
            scores.append(dot(key, query, TN))
        for (pix, head), score in zip(units, scores):
            score = jnp.where(keep[pix * 128 : pix * 128 + 128], score * 0.25, -1e30)
            powered = jnp.exp(score - jnp.max(score, axis=0, keepdims=True))
            full.append(powered * (1.0 / jnp.sum(powered, axis=0, keepdims=True)))
        for (pix, head), prob in zip(units, full):
            probs[pix, head] = prob
            at = pl.multiple_of(head * 16, 16)
            cols = pl.ds(pix * 128, 128)
            value = proj_t[pl.ds(512 + at, 16), cols]
            att_t[pl.ds(at, 16), cols] = dot(value, prob.astype(BF16)).astype(BF16)
        return carry

    lax.fori_loop(0, HEADS // BATCH, attend, 0)

    for copy in copies[2:]:
        copy.wait()
    gain_second = gain_second_ref[...]
    attended_t = att_t[...]
    out_w = out_w_ref[...]
    residual = inputs + dot(attended_t, out_w, TN)
    normed_two, inverse_two = norm_rows(residual)
    second_in = (normed_two * gain_second).astype(BF16)
    back = jnp.zeros((256, 256), F32)
    for part in range(4):
        cols = pl.ds(part * 256, 256)
        up_part = up_ref[:, cols]
        pre = dot(second_in, up_part)
        tangent = jnp.tanh(GELU_C * (pre + GELU_A * pre * pre * pre))
        activated = (0.5 * pre * (1.0 + tangent)).astype(BF16)
        slope = 0.5 * (1.0 + tangent) + 0.5 * pre * (1.0 - tangent * tangent) * GELU_C * (
            1.0 + 3.0 * GELU_A * pre * pre
        )
        put(4 + part, slice(0, 256), dot(activated, upstream, TN))
        hidden_grad = (dot(upstream, down_ref[cols, :], NT) * slope).astype(BF16)
        put(part, slice(0, 256), dot(second_in, hidden_grad, TN))
        back = back + dot(hidden_grad, up_part, NT)
    resid_grad = upstream.astype(F32) + norm_back(normed_two, inverse_two, gain_second, back)
    resid_half = resid_grad.astype(BF16)
    out_grad = dot(attended_t, resid_half)
    put(6, slice(256, 384), out_grad[:, :128])
    put(7, slice(256, 384), out_grad[:, 128:])
    att_grad_t[...] = dot(out_w, resid_half, NT).astype(BF16)

    def attend_back(batch, carry):
        units = [(pix, batch * BATCH + step) for step in range(BATCH) for pix in range(2)]
        prob_grads, score_grads, outs = [], [], []
        for pix, head in units:
            at = pl.multiple_of(head * 16, 16)
            cols = pl.ds(pix * 128, 128)
            value = proj_t[pl.ds(512 + at, 16), cols]
            prob_grads.append(dot(value, att_grad_t[pl.ds(at, 16), cols], TN))
        for (pix, head), prob_grad in zip(units, prob_grads):
            full = probs[pix, head]
            total = jnp.sum(full * prob_grad, axis=0, keepdims=True)
            score_grads.append((full * (prob_grad - total) * 0.25).astype(BF16))
        for (pix, head), score_grad in zip(units, score_grads):
            at = pl.multiple_of(head * 16, 16)
            cols = pl.ds(pix * 128, 128)
            query = proj_t[pl.ds(at, 16), cols]
            key = proj_t[pl.ds(256 + at, 16), cols]
            grad = att_grad_t[pl.ds(at, 16), cols]
            outs.append(
                (
                    dot(key, score_grad),
                    dot(score_grad, query, NT),
                    dot(probs[pix, head].astype(BF16), grad, NT),
                )
            )
        for (pix, head), got in zip(units, outs):
            at = pl.multiple_of(head * 16, 16)
            cols = pl.ds(pix * 128, 128)
            proj_grad_t[pl.ds(at, 16), cols] = got[0].astype(BF16)
            proj_grad_t[pl.ds(256 + at, 16), cols] = got[1].T.astype(BF16)
            proj_grad_t[pl.ds(512 + at, 16), cols] = got[2].T.astype(BF16)
        return carry

    lax.fori_loop(0, HEADS // BATCH, attend_back, 0)

    grad_t = proj_grad_t[...]
    first_t = first_in.T
    for part in range(3):
        qkv_grad = dot(first_t, grad_t[part * 256 : part * 256 + 256], NT)
        put(2 * part, slice(256, 384), qkv_grad[:, :128])
        put(2 * part + 1, slice(256, 384), qkv_grad[:, 128:])
    first_back = dot(grad_t, qkv_ref[...], ((0,), (1,)))
    grad = resid_grad + norm_back(normed_one, inverse_one, gain_first, first_back)
    grad = jnp.where(keep, grad, 0.0).astype(BF16)
    slot = iota((256, 256), 0)
    want = slot // 4 % 2 * 128 + slot // 8 * 4 + slot % 4
    grad_ref[...] = dot((iota((256, 256), 1) == want).astype(BF16), grad).astype(BF16)
    for at, sent_ref in enumerate(sent_refs):
        sent_ref[...] = terms_ref[at // 4, at % 4]


def core_sum_kernel(mine_ref, other_ref, out_ref):
    out_ref[...] = (mine_ref[...].astype(F32) + other_ref[...].astype(F32)).astype(BF16)


def x_sum_kernel(mine_ref, other_ref, one_ref, two_ref, three_ref, grad_ref, out_ref):
    total = mine_ref[...].astype(F32) + other_ref[...].astype(F32)
    total = total + one_ref[...].astype(F32)
    total = total + two_ref[...].astype(F32) + three_ref[...].astype(F32)
    out_ref[:, :, 0:384] = total.astype(BF16).reshape(32, 8, 384)
    out_ref[:, :, 384:640] = grad_ref[...].reshape(32, 8, 256)


def yz_sum_kernel(joint_ref, total_ref):
    total = jnp.sum(joint_ref[:, :, 0:384].astype(F32), axis=0).astype(BF16)
    total_ref[...] = jnp.broadcast_to(total[None], total_ref.shape)


def expand_kernel(joint_ref, match_ref, out_ref):
    for group in range(2):
        back = joint_ref[group * 16 : group * 16 + 16, :, 384:640].reshape(128, 256)
        out_ref[pl.ds(group * 256, 256), :] = dot(match_ref[group], back, TN).astype(BF16)


def spread_kernel(pieces, *refs):
    count = len(pieces)
    held = refs[:count]
    qkv_hbm, out_hbm, up_hbm, down_hbm, wide, narrow, sent = refs[-7:]
    core, place = lax.axis_index("c"), lax.axis_index("x")

    def each(act):
        for at, (hops, flip) in enumerate(pieces):
            pair = lax.rem(place - hops + 4, 4)
            group = 2 * pair + (core ^ flip)

            def move(test, source, target, sem):
                @pl.when(test)
                def _():
                    act(pltpu.make_async_copy(source.at[at], target(), sent.at[at, sem]))

            def across(ref, first, size):
                return lambda: ref.at[:, pl.ds(pl.multiple_of((group - first) * size, size), size)]

            def along():
                return down_hbm.at[pl.ds(pl.multiple_of((group - 4) * 256, 256), 256), :]

            if act is start:
                piece = held[at][...].astype(F32)
                wide[at] = piece[:, :256]
                narrow[at] = piece[:, 256:]
            move(pair < 2, wide, across(up_hbm, 0, 256), 0)
            move(pair >= 2, wide, along, 0)
            move(pair < 3, narrow, across(qkv_hbm, 0, 128), 1)
            move(pair >= 3, narrow, across(out_hbm, 6, 128), 1)

    def start(copy):
        copy.start()

    def wait(copy):
        copy.wait()

    each(start)
    each(wait)


def spread(pieces, held, outs=()):
    shape = jax.ShapeDtypeStruct
    kept = pl.BlockSpec(memory_space=pl.ANY)
    count = len(pieces)
    return pl.pallas_call(
        functools.partial(spread_kernel, pieces),
        out_shape=(
            shape((256, 768), F32),
            shape((256, 256), F32),
            shape((256, 1024), F32),
            shape((1024, 256), F32),
        ),
        in_specs=[pl.BlockSpec(memory_space=pltpu.VMEM)] * count + [kept] * len(outs),
        out_specs=[kept] * 4,
        scratch_shapes=[
            pltpu.VMEM((count, 256, 256), F32),
            pltpu.VMEM((count, 256, 128), F32),
            pltpu.SemaphoreType.DMA((count, 2)),
        ],
        input_output_aliases={at + count: at for at in range(len(outs))},
        compiler_params=pltpu.CompilerParams(vmem_limit_bytes=VMEM_LIMIT),
        cost_estimate=pl.CostEstimate(flops=0, bytes_accessed=2000000, transcendentals=0),
    )(*held, *outs)


def stay(array):
    return pltpu.with_memory_space_constraint(array, pltpu.HBM)


def run(kernel, out_shape, *args, scratch=(), held=(), cost=None):
    specs = [
        pl.BlockSpec(memory_space=pltpu.HBM if at in held else pltpu.VMEM)
        for at in range(len(args))
    ]
    args = [stay(array) if at in held else array for at, array in enumerate(args)]
    return pl.pallas_call(
        kernel,
        out_shape=out_shape,
        in_specs=specs,
        scratch_shapes=list(scratch),
        compiler_params=pltpu.CompilerParams(vmem_limit_bytes=VMEM_LIMIT),
        cost_estimate=cost
        and pl.CostEstimate(flops=0, bytes_accessed=cost, transcendentals=0),
    )(*args)


def shift(array, axis, size, by):
    return lax.ppermute(array, axis, [(at, (at + by) % size) for at in range(size)])


def per_device(
    features,
    cotangent,
    valid_dates,
    gain_first,
    qkv_weight,
    out_weight,
    gain_second,
    up_weight,
    down_weight,
):
    shape = jax.ShapeDtypeStruct
    width = features.shape[-1]
    scale = float(256 * 2 * 256) ** (-0.5)
    dates = ("y", "z")
    with jax.named_scope("compact"):
        send, match = run(
            compact_kernel,
            (shape((512, width), BF16), shape((2, 128, 256), BF16)),
            features.reshape(512, width),
            cotangent.reshape(512, width),
            valid_dates.T,
            held=(0, 1, 2),
            scratch=(
                pltpu.VMEM((512, width), BF16),
                pltpu.VMEM((512, width), BF16),
                pltpu.VMEM((8, 32), jnp.int32),
                pltpu.SemaphoreType.DMA((3,)),
            ),
        )
    with jax.named_scope("to_owner"):
        recv = lax.all_to_all(
            send.reshape(32, 16, width), dates, split_axis=0, concat_axis=0, tiled=True
        )
    piece = shape((256, 384), BF16)
    with jax.named_scope("layer"):
        grad, *terms = run(
            functools.partial(layer_kernel, scale),
            (shape((256, width), BF16),) + (piece,) * 8,
            recv.reshape(512, width),
            gain_first.reshape(1, width),
            qkv_weight,
            out_weight,
            gain_second.reshape(1, width),
            up_weight,
            down_weight,
            held=range(1, 7),
            scratch=(
                pltpu.VMEM((1, width), F32),
                pltpu.VMEM((256, 768), BF16),
                pltpu.VMEM((256, 256), BF16),
                pltpu.VMEM((1, width), F32),
                pltpu.VMEM((256, 1024), BF16),
                pltpu.VMEM((1024, 256), BF16),
                pltpu.SemaphoreType.DMA((6,)),
                pltpu.VMEM((2, HEADS, 128, 128), F32),
                pltpu.VMEM((768, 256), BF16),
                pltpu.VMEM((256, 256), BF16),
                pltpu.VMEM((256, 256), BF16),
                pltpu.VMEM((768, 256), BF16),
                pltpu.VMEM((2, 4, 256, 384), BF16),
            ),
        )
    with jax.named_scope("core_sum"):
        other = {by: shift(terms[4 + by], "c", 2, 1) for by in (3, 1, 2, 0)}
        slots = {by: run(core_sum_kernel, piece, terms[by], other[by]) for by in (3, 1, 2)}
    with jax.named_scope("x_sum"):
        got = [shift(slots[by], "x", 4, by) for by in (3, 1, 2)]
        joint = run(x_sum_kernel, shape((32, 8, 640), BF16), terms[0], other[0], *got, grad)
    with jax.named_scope("yz_sum"):
        joint = lax.all_to_all(joint, dates, split_axis=0, concat_axis=0, tiled=True)
        total = run(yz_sum_kernel, shape((32, 8, 384), BF16), joint)
    with jax.named_scope("yz_gather"):
        part = lax.all_to_all(total, dates, split_axis=0, concat_axis=0, tiled=True)
        part = part.reshape(256, 384)
        joint, _ = lax.optimization_barrier((joint, part))
    with jax.named_scope("x_gather"):
        near = {by: shift(part, "x", 4, by) for by in (2, 1, 3)}
        part_far = shift(part, "c", 2, 1)
    with jax.named_scope("expand"):
        feature_grad = run(
            expand_kernel, shape((512, width), BF16), joint, match, cost=1000000
        )
    with jax.named_scope("spread"):
        outs = spread(((0, 0), (0, 1)), (part, part_far))
    with jax.named_scope("core_gather"):
        near, feature_grad, outs = lax.optimization_barrier((near, feature_grad, outs))
        far = {by: shift(near[by], "c", 2, 1) for by in (2, 1, 3)}
    with jax.named_scope("spread"):
        outs = spread(((2, 0), (1, 0), (3, 0)), [near[by] for by in (2, 1, 3)], outs)
        outs = spread(((2, 1), (1, 1), (3, 1)), [far[by] for by in (2, 1, 3)], outs)
    return (feature_grad.reshape(features.shape), *outs)


def solution(mesh):
    fine = Mesh(mesh.devices.reshape(4, 8, 4, 2), ("y", "z", "x", "c"))
    dates, tiles = ("y", "z"), ("x", "c")
    in_specs = (
        P(tiles, None, dates, None),
        P(tiles, None, dates, None),
        P(tiles, dates),
        P(),
        P(),
        P(),
        P(),
        P(),
        P(),
    )
    out_specs = (P(tiles, None, dates, None), P(), P(), P(), P())
    return jax.shard_map(
        per_device, mesh=fine, in_specs=in_specs, out_specs=out_specs, check_vma=False
    )
```

```python
import functools

import jax
import jax.numpy as jnp
from jax import lax
from jax.experimental import pallas as pl
from jax.experimental.pallas import tpu as pltpu
from jax.sharding import Mesh
from jax.sharding import PartitionSpec as P

HEADS = 16
BATCH = 16
ORDER = (2, 1, 3)
EPS = 1e-05
GELU_C = 0.7978845608028654
GELU_A = 0.044715
ABSENT = 2.0**100

F32 = jnp.float32
BF16 = jnp.bfloat16
VMEM_LIMIT = 48 * 1024 * 1024


def iota(shape, axis):
    return lax.broadcasted_iota(jnp.int32, shape, axis)


def dot(left, right, dims=((1,), (0,))):
    return lax.dot_general(left, right, (dims, ((), ())), preferred_element_type=F32)


TN = ((0,), (0,))
NT = ((1,), (1,))


def slot_matrix(valid, group):
    date = iota((8, 256), 1) % 8
    day = iota((8, 256), 0)
    held = valid.astype(F32)
    keep_all = dot(held, (day == date).astype(F32), TN)
    rank_all = dot(held, (day < date).astype(F32), TN)
    own = iota((32, 256), 0) == iota((32, 256), 1) // 16 + group * 16
    keep = jnp.sum(jnp.where(own, keep_all, 0.0), axis=0, keepdims=True)
    rank = jnp.sum(jnp.where(own, rank_all, 0.0), axis=0, keepdims=True)
    shape = (256, 256)
    row, col = iota(shape, 0), iota(shape, 1)
    match = (
        (row // 16 == col // 16)
        & ((row // 4) % 2 == (col // 8) % 2)
        & (rank == (row % 4).astype(F32))
        & (keep > 0.5)
    )
    return match.astype(F32)


def compact_kernel(feat_hbm, cot_hbm, valid_hbm, send_ref, match_ref, feat, cot, valid_ref, arrived):
    copies = [
        pltpu.make_async_copy(valid_hbm, valid_ref, arrived.at[0]),
        pltpu.make_async_copy(feat_hbm, feat, arrived.at[1]),
        pltpu.make_async_copy(cot_hbm, cot, arrived.at[2]),
    ]
    for copy in copies:
        copy.start()
    copies[0].wait()
    valid = valid_ref[...]
    is_feat = (iota((256, 1), 0) // 8) % 2 == 0
    picks = []
    for group in range(2):
        match = slot_matrix(valid, group)
        pick_feat = jnp.where(is_feat, match, 0.0).astype(BF16)
        pick_cot = jnp.where(is_feat, 0.0, match).astype(BF16)
        filled = jnp.sum(match, axis=1, keepdims=True) > 0.5
        match_ref[group] = match.reshape(16, 16, 256)[:, :8].reshape(128, 256).astype(BF16)
        picks.append((pick_feat, pick_cot, is_feat & jnp.logical_not(filled)))
    copies[1].wait()
    copies[2].wait()
    for group, (pick_feat, pick_cot, absent) in enumerate(picks):
        rows = pl.ds(group * 256, 256)
        got = dot(pick_feat, feat[rows, :]) + dot(pick_cot, cot[rows, :])
        send_ref[rows, :] = jnp.where(absent, ABSENT, got).astype(BF16)


def row_mean(values):
    return jnp.sum(values, axis=-1, keepdims=True) * (1.0 / values.shape[-1])


def norm_rows(hidden):
    centre = hidden - row_mean(hidden)
    inverse = lax.rsqrt(row_mean(centre * centre) + EPS)
    return centre * inverse, inverse


def norm_back(normed, inverse, gain, upstream):
    scaled = upstream * gain
    return inverse * (scaled - row_mean(scaled) - normed * row_mean(scaled * normed))


def layer_kernel(
    scale,
    recv_ref,
    gain_first_hbm,
    qkv_hbm,
    out_w_hbm,
    gain_second_hbm,
    up_hbm,
    down_hbm,
    grad_ref,
    *rest,
):
    (*sent_refs, gain_first_ref, qkv_ref, out_w_ref, gain_second_ref, up_ref, down_ref) = rest[:14]
    arrived, probs, proj_t, att_t, att_grad_t, proj_grad_t, terms_ref = rest[14:]
    pairs = (
        (qkv_hbm, qkv_ref),
        (gain_first_hbm, gain_first_ref),
        (out_w_hbm, out_w_ref),
        (gain_second_hbm, gain_second_ref),
        (up_hbm, up_ref),
        (down_hbm, down_ref),
    )
    copies = [
        pltpu.make_async_copy(held, ref, arrived.at[at]) for at, (held, ref) in enumerate(pairs)
    ]
    for copy in copies:
        copy.start()
    core = lax.axis_index("c")
    place = lax.axis_index("x")

    def put(group, columns, value):
        slot = lax.rem(group // 2 - place + 4, 4)
        terms_ref[(group % 2) ^ core, slot, :, columns] = (value * scale).astype(BF16)

    token = iota((256, 512), 0)
    target = (token % 128) // 4 * 16 + token // 128 * 4 + token % 4
    source = iota((256, 512), 1)
    recv = recv_ref[...]
    inputs = dot((source == target).astype(BF16), recv)
    upstream = dot((source == target + 8).astype(BF16), recv).astype(BF16)
    keep = inputs[:, 0:1] < 0.5 * ABSENT
    inputs = jnp.where(keep, inputs, 0.0)
    normed_one, inverse_one = norm_rows(inputs)
    copies[0].wait()
    copies[1].wait()
    gain_first = gain_first_ref[...]
    first_in = (normed_one * gain_first).astype(BF16)
    proj_t[...] = dot(qkv_ref[...], first_in, ((0,), (1,))).astype(BF16)

    def attend(batch, carry):
        units = [(pix, batch * BATCH + step) for step in range(BATCH) for pix in range(2)]
        scores, full = [], []
        for pix, head in units:
            at = pl.multiple_of(head * 16, 16)
            cols = pl.ds(pix * 128, 128)
            query = proj_t[pl.ds(at, 16), cols]
            key = proj_t[pl.ds(256 + at, 16), cols]
            scores.append(dot(key, query, TN))
        for (pix, head), score in zip(units, scores):
            score = jnp.where(keep[pix * 128 : pix * 128 + 128], score * 0.25, -1e30)
            powered = jnp.exp(score - jnp.max(score, axis=0, keepdims=True))
            full.append(powered * (1.0 / jnp.sum(powered, axis=0, keepdims=True)))
        for (pix, head), prob in zip(units, full):
            probs[pix, head] = prob
            at = pl.multiple_of(head * 16, 16)
            cols = pl.ds(pix * 128, 128)
            value = proj_t[pl.ds(512 + at, 16), cols]
            att_t[pl.ds(at, 16), cols] = dot(value, prob.astype(BF16)).astype(BF16)
        return carry

    lax.fori_loop(0, HEADS // BATCH, attend, 0)

    for copy in copies[2:]:
        copy.wait()
    gain_second = gain_second_ref[...]
    attended_t = att_t[...]
    out_w = out_w_ref[...]
    residual = inputs + dot(attended_t, out_w, TN)
    normed_two, inverse_two = norm_rows(residual)
    second_in = (normed_two * gain_second).astype(BF16)
    back = jnp.zeros((256, 256), F32)
    for part in range(4):
        cols = pl.ds(part * 256, 256)
        up_part = up_ref[:, cols]
        pre = dot(second_in, up_part)
        tangent = jnp.tanh(GELU_C * (pre + GELU_A * pre * pre * pre))
        activated = (0.5 * pre * (1.0 + tangent)).astype(BF16)
        slope = 0.5 * (1.0 + tangent) + 0.5 * pre * (1.0 - tangent * tangent) * GELU_C * (
            1.0 + 3.0 * GELU_A * pre * pre
        )
        put(4 + part, slice(0, 256), dot(activated, upstream, TN))
        hidden_grad = (dot(upstream, down_ref[cols, :], NT) * slope).astype(BF16)
        put(part, slice(0, 256), dot(second_in, hidden_grad, TN))
        back = back + dot(hidden_grad, up_part, NT)
    resid_grad = upstream.astype(F32) + norm_back(normed_two, inverse_two, gain_second, back)
    resid_half = resid_grad.astype(BF16)
    out_grad = dot(attended_t, resid_half)
    put(6, slice(256, 384), out_grad[:, :128])
    put(7, slice(256, 384), out_grad[:, 128:])
    att_grad_t[...] = dot(out_w, resid_half, NT).astype(BF16)

    def attend_back(batch, carry):
        units = [(pix, batch * BATCH + step) for step in range(BATCH) for pix in range(2)]
        prob_grads, score_grads, outs = [], [], []
        for pix, head in units:
            at = pl.multiple_of(head * 16, 16)
            cols = pl.ds(pix * 128, 128)
            value = proj_t[pl.ds(512 + at, 16), cols]
            prob_grads.append(dot(value, att_grad_t[pl.ds(at, 16), cols], TN))
        for (pix, head), prob_grad in zip(units, prob_grads):
            full = probs[pix, head]
            total = jnp.sum(full * prob_grad, axis=0, keepdims=True)
            score_grads.append((full * (prob_grad - total) * 0.25).astype(BF16))
        for (pix, head), score_grad in zip(units, score_grads):
            at = pl.multiple_of(head * 16, 16)
            cols = pl.ds(pix * 128, 128)
            query = proj_t[pl.ds(at, 16), cols]
            key = proj_t[pl.ds(256 + at, 16), cols]
            grad = att_grad_t[pl.ds(at, 16), cols]
            outs.append(
                (
                    dot(key, score_grad),
                    dot(score_grad, query, NT),
                    dot(probs[pix, head].astype(BF16), grad, NT),
                )
            )
        for (pix, head), got in zip(units, outs):
            at = pl.multiple_of(head * 16, 16)
            cols = pl.ds(pix * 128, 128)
            proj_grad_t[pl.ds(at, 16), cols] = got[0].astype(BF16)
            proj_grad_t[pl.ds(256 + at, 16), cols] = got[1].T.astype(BF16)
            proj_grad_t[pl.ds(512 + at, 16), cols] = got[2].T.astype(BF16)
        return carry

    lax.fori_loop(0, HEADS // BATCH, attend_back, 0)

    grad_t = proj_grad_t[...]
    first_t = first_in.T
    for part in range(3):
        qkv_grad = dot(first_t, grad_t[part * 256 : part * 256 + 256], NT)
        put(2 * part, slice(256, 384), qkv_grad[:, :128])
        put(2 * part + 1, slice(256, 384), qkv_grad[:, 128:])
    first_back = dot(grad_t, qkv_ref[...], ((0,), (1,)))
    grad = resid_grad + norm_back(normed_one, inverse_one, gain_first, first_back)
    grad = jnp.where(keep, grad, 0.0).astype(BF16)
    slot = iota((256, 256), 0)
    want = slot // 4 % 2 * 128 + slot // 8 * 4 + slot % 4
    grad_ref[...] = dot((iota((256, 256), 1) == want).astype(BF16), grad).astype(BF16)
    for at, sent_ref in enumerate(sent_refs):
        sent_ref[...] = terms_ref[at // 4, at % 4]


def core_sum_kernel(mine_ref, other_ref, out_ref):
    out_ref[...] = (mine_ref[...].astype(F32) + other_ref[...].astype(F32)).astype(BF16)


def x_sum_kernel(mine_ref, other_ref, one_ref, two_ref, three_ref, grad_ref, out_ref):
    total = mine_ref[...].astype(F32) + other_ref[...].astype(F32)
    total = total + one_ref[...].astype(F32)
    total = total + two_ref[...].astype(F32) + three_ref[...].astype(F32)
    out_ref[:, :, 0:384] = total.astype(BF16).reshape(32, 8, 384)
    out_ref[:, :, 384:640] = grad_ref[...].reshape(32, 8, 256)


def yz_sum_kernel(joint_ref, total_ref):
    total = jnp.sum(joint_ref[:, :, 0:384].astype(F32), axis=0).astype(BF16)
    total_ref[...] = jnp.broadcast_to(total[None], total_ref.shape)


def expand_kernel(joint_ref, match_ref, out_ref):
    for group in range(2):
        back = joint_ref[group * 16 : group * 16 + 16, :, 384:640].reshape(128, 256)
        out_ref[pl.ds(group * 256, 256), :] = dot(match_ref[group], back, TN).astype(BF16)


def spread_kernel(pieces, *refs):
    count = len(pieces)
    held = refs[:count]
    qkv_hbm, out_hbm, up_hbm, down_hbm, wide, narrow, sent = refs[-7:]
    core, place = lax.axis_index("c"), lax.axis_index("x")

    def each(act):
        for at, (hops, flip) in enumerate(pieces):
            pair = lax.rem(place - hops + 4, 4)
            group = 2 * pair + (core ^ flip)

            def move(test, source, target, sem):
                @pl.when(test)
                def _():
                    act(pltpu.make_async_copy(source.at[at], target(), sent.at[at, sem]))

            def across(ref, first, size):
                return lambda: ref.at[:, pl.ds(pl.multiple_of((group - first) * size, size), size)]

            def along():
                return down_hbm.at[pl.ds(pl.multiple_of((group - 4) * 256, 256), 256), :]

            if act is start:
                piece = held[at][...].astype(F32)
                wide[at] = piece[:, :256]
                narrow[at] = piece[:, 256:]
            move(pair < 2, wide, across(up_hbm, 0, 256), 0)
            move(pair >= 2, wide, along, 0)
            move(pair < 3, narrow, across(qkv_hbm, 0, 128), 1)
            move(pair >= 3, narrow, across(out_hbm, 6, 128), 1)

    def start(copy):
        copy.start()

    def wait(copy):
        copy.wait()

    each(start)
    each(wait)


def spread(pieces, held, outs=()):
    shape = jax.ShapeDtypeStruct
    kept = pl.BlockSpec(memory_space=pl.ANY)
    count = len(pieces)
    return pl.pallas_call(
        functools.partial(spread_kernel, pieces),
        out_shape=(
            shape((256, 768), F32),
            shape((256, 256), F32),
            shape((256, 1024), F32),
            shape((1024, 256), F32),
        ),
        in_specs=[pl.BlockSpec(memory_space=pltpu.VMEM)] * count + [kept] * len(outs),
        out_specs=[kept] * 4,
        scratch_shapes=[
            pltpu.VMEM((count, 256, 256), F32),
            pltpu.VMEM((count, 256, 128), F32),
            pltpu.SemaphoreType.DMA((count, 2)),
        ],
        input_output_aliases={at + count: at for at in range(len(outs))},
        compiler_params=pltpu.CompilerParams(vmem_limit_bytes=VMEM_LIMIT),
        cost_estimate=pl.CostEstimate(flops=0, bytes_accessed=2000000, transcendentals=0),
    )(*held, *outs)


def stay(array):
    return pltpu.with_memory_space_constraint(array, pltpu.HBM)


def run(kernel, out_shape, *args, scratch=(), held=(), cost=None):
    specs = [
        pl.BlockSpec(memory_space=pltpu.HBM if at in held else pltpu.VMEM)
        for at in range(len(args))
    ]
    args = [stay(array) if at in held else array for at, array in enumerate(args)]
    return pl.pallas_call(
        kernel,
        out_shape=out_shape,
        in_specs=specs,
        scratch_shapes=list(scratch),
        compiler_params=pltpu.CompilerParams(vmem_limit_bytes=VMEM_LIMIT),
        cost_estimate=cost
        and pl.CostEstimate(flops=0, bytes_accessed=cost, transcendentals=0),
    )(*args)


def shift(array, axis, size, by):
    return lax.ppermute(array, axis, [(at, (at + by) % size) for at in range(size)])


def per_device(
    features,
    cotangent,
    valid_dates,
    gain_first,
    qkv_weight,
    out_weight,
    gain_second,
    up_weight,
    down_weight,
):
    shape = jax.ShapeDtypeStruct
    width = features.shape[-1]
    scale = float(256 * 2 * 256) ** (-0.5)
    dates = ("y", "z")
    with jax.named_scope("compact"):
        send, match = run(
            compact_kernel,
            (shape((512, width), BF16), shape((2, 128, 256), BF16)),
            features.reshape(512, width),
            cotangent.reshape(512, width),
            valid_dates.T,
            held=(0, 1, 2),
            scratch=(
                pltpu.VMEM((512, width), BF16),
                pltpu.VMEM((512, width), BF16),
                pltpu.VMEM((8, 32), jnp.int32),
                pltpu.SemaphoreType.DMA((3,)),
            ),
        )
    with jax.named_scope("to_owner"):
        recv = lax.all_to_all(
            send.reshape(32, 16, width), dates, split_axis=0, concat_axis=0, tiled=True
        )
    piece = shape((256, 384), BF16)
    with jax.named_scope("layer"):
        grad, *terms = run(
            functools.partial(layer_kernel, scale),
            (shape((256, width), BF16),) + (piece,) * 8,
            recv.reshape(512, width),
            gain_first.reshape(1, width),
            qkv_weight,
            out_weight,
            gain_second.reshape(1, width),
            up_weight,
            down_weight,
            held=range(1, 7),
            scratch=(
                pltpu.VMEM((1, width), F32),
                pltpu.VMEM((256, 768), BF16),
                pltpu.VMEM((256, 256), BF16),
                pltpu.VMEM((1, width), F32),
                pltpu.VMEM((256, 1024), BF16),
                pltpu.VMEM((1024, 256), BF16),
                pltpu.SemaphoreType.DMA((6,)),
                pltpu.VMEM((2, HEADS, 128, 128), F32),
                pltpu.VMEM((768, 256), BF16),
                pltpu.VMEM((256, 256), BF16),
                pltpu.VMEM((256, 256), BF16),
                pltpu.VMEM((768, 256), BF16),
                pltpu.VMEM((2, 4, 256, 384), BF16),
            ),
        )
    with jax.named_scope("core_sum"):
        other = {by: shift(terms[4 + by], "c", 2, 1) for by in (3, 1, 2, 0)}
        slots = {by: run(core_sum_kernel, piece, terms[by], other[by]) for by in (3, 1, 2)}
    with jax.named_scope("x_sum"):
        got = [shift(slots[by], "x", 4, by) for by in (3, 1, 2)]
        joint = run(x_sum_kernel, shape((32, 8, 640), BF16), terms[0], other[0], *got, grad)
    with jax.named_scope("yz_sum"):
        joint = lax.all_to_all(joint, dates, split_axis=0, concat_axis=0, tiled=True)
        total = run(yz_sum_kernel, shape((32, 8, 384), BF16), joint)
    with jax.named_scope("yz_gather"):
        part = lax.all_to_all(total, dates, split_axis=0, concat_axis=0, tiled=True)
        part = part.reshape(256, 384)
        joint, _ = lax.optimization_barrier((joint, part))
    with jax.named_scope("x_gather"):
        near = [shift(part, "x", 4, by) for by in ORDER]
        part_far = shift(part, "c", 2, 1)
    with jax.named_scope("expand"):
        feature_grad = run(
            expand_kernel, shape((512, width), BF16), joint, match, cost=1000000
        )
    with jax.named_scope("spread"):
        outs = spread(((0, 0), (0, 1)), (part, part_far))
    with jax.named_scope("core_gather"):
        near, feature_grad, outs = lax.optimization_barrier((near, feature_grad, outs))
        far = [shift(got, "c", 2, 1) for got in near]
    with jax.named_scope("spread"):
        outs = spread([(by, 0) for by in ORDER], near, outs)
        outs = spread([(by, 1) for by in ORDER], far, outs)
    return (feature_grad.reshape(features.shape), *outs)


def solution(mesh):
    fine = Mesh(mesh.devices.reshape(4, 8, 4, 2), ("y", "z", "x", "c"))
    dates, tiles = ("y", "z"), ("x", "c")
    in_specs = (
        P(tiles, None, dates, None),
        P(tiles, None, dates, None),
        P(tiles, dates),
        P(),
        P(),
        P(),
        P(),
        P(),
        P(),
    )
    out_specs = (P(tiles, None, dates, None), P(), P(), P(), P())
    return jax.shard_map(
        per_device, mesh=fine, in_specs=in_specs, out_specs=out_specs, check_vma=False
    )
```

```python
import functools

import jax
import jax.numpy as jnp
from jax import lax
from jax.experimental import pallas as pl
from jax.experimental.pallas import tpu as pltpu
from jax.sharding import Mesh
from jax.sharding import PartitionSpec as P

HEADS = 16
BATCH = 16
EPS = 1e-05
GELU_C = 0.7978845608028654
GELU_A = 0.044715
ABSENT = 2.0**100

F32 = jnp.float32
BF16 = jnp.bfloat16
VMEM_LIMIT = 48 * 1024 * 1024


def iota(shape, axis):
    return lax.broadcasted_iota(jnp.int32, shape, axis)


def dot(left, right, dims=((1,), (0,))):
    return lax.dot_general(left, right, (dims, ((), ())), preferred_element_type=F32)


TN = ((0,), (0,))
NT = ((1,), (1,))


def slot_matrix(valid, group):
    date = iota((8, 256), 1) % 8
    day = iota((8, 256), 0)
    held = valid.astype(F32)
    keep_all = dot(held, (day == date).astype(F32), TN)
    rank_all = dot(held, (day < date).astype(F32), TN)
    own = iota((32, 256), 0) == iota((32, 256), 1) // 16 + group * 16
    keep = jnp.sum(jnp.where(own, keep_all, 0.0), axis=0, keepdims=True)
    rank = jnp.sum(jnp.where(own, rank_all, 0.0), axis=0, keepdims=True)
    shape = (256, 256)
    row, col = iota(shape, 0), iota(shape, 1)
    match = (
        (row // 16 == col // 16)
        & ((row // 4) % 2 == (col // 8) % 2)
        & (rank == (row % 4).astype(F32))
        & (keep > 0.5)
    )
    return match.astype(F32)


def compact_kernel(feat_hbm, cot_hbm, valid_hbm, send_ref, match_ref, feat, cot, valid_ref, arrived):
    copies = [
        pltpu.make_async_copy(valid_hbm, valid_ref, arrived.at[0]),
        pltpu.make_async_copy(feat_hbm, feat, arrived.at[1]),
        pltpu.make_async_copy(cot_hbm, cot, arrived.at[2]),
    ]
    for copy in copies:
        copy.start()
    copies[0].wait()
    valid = valid_ref[...]
    is_feat = (iota((256, 1), 0) // 8) % 2 == 0
    picks = []
    for group in range(2):
        match = slot_matrix(valid, group)
        pick_feat = jnp.where(is_feat, match, 0.0).astype(BF16)
        pick_cot = jnp.where(is_feat, 0.0, match).astype(BF16)
        filled = jnp.sum(match, axis=1, keepdims=True) > 0.5
        match_ref[group] = match.reshape(16, 16, 256)[:, :8].reshape(128, 256).astype(BF16)
        picks.append((pick_feat, pick_cot, is_feat & jnp.logical_not(filled)))
    copies[1].wait()
    copies[2].wait()
    for group, (pick_feat, pick_cot, absent) in enumerate(picks):
        rows = pl.ds(group * 256, 256)
        got = dot(pick_feat, feat[rows, :]) + dot(pick_cot, cot[rows, :])
        send_ref[rows, :] = jnp.where(absent, ABSENT, got).astype(BF16)


def row_mean(values):
    return jnp.sum(values, axis=-1, keepdims=True) * (1.0 / values.shape[-1])


def norm_rows(hidden):
    centre = hidden - row_mean(hidden)
    inverse = lax.rsqrt(row_mean(centre * centre) + EPS)
    return centre * inverse, inverse


def norm_back(normed, inverse, gain, upstream):
    scaled = upstream * gain
    return inverse * (scaled - row_mean(scaled) - normed * row_mean(scaled * normed))


def layer_kernel(
    scale,
    recv_ref,
    gain_first_hbm,
    qkv_hbm,
    out_w_hbm,
    gain_second_hbm,
    up_hbm,
    down_hbm,
    grad_ref,
    *rest,
):
    (*sent_refs, gain_first_ref, qkv_ref, out_w_ref, gain_second_ref, up_ref, down_ref) = rest[:14]
    arrived, probs, proj_t, att_t, att_grad_t, proj_grad_t, terms_ref = rest[14:]
    pairs = (
        (qkv_hbm, qkv_ref),
        (gain_first_hbm, gain_first_ref),
        (out_w_hbm, out_w_ref),
        (gain_second_hbm, gain_second_ref),
        (up_hbm, up_ref),
        (down_hbm, down_ref),
    )
    copies = [
        pltpu.make_async_copy(held, ref, arrived.at[at]) for at, (held, ref) in enumerate(pairs)
    ]
    for copy in copies:
        copy.start()
    core = lax.axis_index("c")
    place = lax.axis_index("x")

    def put(group, columns, value):
        slot = lax.rem(group // 2 - place + 4, 4)
        terms_ref[(group % 2) ^ core, slot, :, columns] = (value * scale).astype(BF16)

    token = iota((256, 512), 0)
    target = (token % 128) // 4 * 16 + token // 128 * 4 + token % 4
    source = iota((256, 512), 1)
    recv = recv_ref[...]
    inputs = dot((source == target).astype(BF16), recv)
    upstream = dot((source == target + 8).astype(BF16), recv).astype(BF16)
    keep = inputs[:, 0:1] < 0.5 * ABSENT
    inputs = jnp.where(keep, inputs, 0.0)
    normed_one, inverse_one = norm_rows(inputs)
    copies[0].wait()
    copies[1].wait()
    gain_first = gain_first_ref[...]
    first_in = (normed_one * gain_first).astype(BF16)
    proj_t[...] = dot(qkv_ref[...], first_in, ((0,), (1,))).astype(BF16)

    def attend(batch, carry):
        units = [(pix, batch * BATCH + step) for step in range(BATCH) for pix in range(2)]
        scores, full = [], []
        for pix, head in units:
            at = pl.multiple_of(head * 16, 16)
            cols = pl.ds(pix * 128, 128)
            query = proj_t[pl.ds(at, 16), cols]
            key = proj_t[pl.ds(256 + at, 16), cols]
            scores.append(dot(key, query, TN))
        for (pix, head), score in zip(units, scores):
            score = jnp.where(keep[pix * 128 : pix * 128 + 128], score * 0.25, -1e30)
            powered = jnp.exp(score - jnp.max(score, axis=0, keepdims=True))
            full.append(powered * (1.0 / jnp.sum(powered, axis=0, keepdims=True)))
        for (pix, head), prob in zip(units, full):
            probs[pix, head] = prob
            at = pl.multiple_of(head * 16, 16)
            cols = pl.ds(pix * 128, 128)
            value = proj_t[pl.ds(512 + at, 16), cols]
            att_t[pl.ds(at, 16), cols] = dot(value, prob.astype(BF16)).astype(BF16)
        return carry

    lax.fori_loop(0, HEADS // BATCH, attend, 0)

    for copy in copies[2:]:
        copy.wait()
    gain_second = gain_second_ref[...]
    attended_t = att_t[...]
    out_w = out_w_ref[...]
    residual = inputs + dot(attended_t, out_w, TN)
    normed_two, inverse_two = norm_rows(residual)
    second_in = (normed_two * gain_second).astype(BF16)
    back = jnp.zeros((256, 256), F32)
    for part in range(4):
        cols = pl.ds(part * 256, 256)
        up_part = up_ref[:, cols]
        pre = dot(second_in, up_part)
        tangent = jnp.tanh(GELU_C * (pre + GELU_A * pre * pre * pre))
        activated = (0.5 * pre * (1.0 + tangent)).astype(BF16)
        slope = 0.5 * (1.0 + tangent) + 0.5 * pre * (1.0 - tangent * tangent) * GELU_C * (
            1.0 + 3.0 * GELU_A * pre * pre
        )
        put(4 + part, slice(0, 256), dot(activated, upstream, TN))
        hidden_grad = (dot(upstream, down_ref[cols, :], NT) * slope).astype(BF16)
        put(part, slice(0, 256), dot(second_in, hidden_grad, TN))
        back = back + dot(hidden_grad, up_part, NT)
    resid_grad = upstream.astype(F32) + norm_back(normed_two, inverse_two, gain_second, back)
    resid_half = resid_grad.astype(BF16)
    out_grad = dot(attended_t, resid_half)
    put(6, slice(256, 384), out_grad[:, :128])
    put(7, slice(256, 384), out_grad[:, 128:])
    att_grad_t[...] = dot(out_w, resid_half, NT).astype(BF16)

    def attend_back(batch, carry):
        units = [(pix, batch * BATCH + step) for step in range(BATCH) for pix in range(2)]
        prob_grads, score_grads, outs = [], [], []
        for pix, head in units:
            at = pl.multiple_of(head * 16, 16)
            cols = pl.ds(pix * 128, 128)
            value = proj_t[pl.ds(512 + at, 16), cols]
            prob_grads.append(dot(value, att_grad_t[pl.ds(at, 16), cols], TN))
        for (pix, head), prob_grad in zip(units, prob_grads):
            full = probs[pix, head]
            total = jnp.sum(full * prob_grad, axis=0, keepdims=True)
            score_grads.append((full * (prob_grad - total) * 0.25).astype(BF16))
        for (pix, head), score_grad in zip(units, score_grads):
            at = pl.multiple_of(head * 16, 16)
            cols = pl.ds(pix * 128, 128)
            query = proj_t[pl.ds(at, 16), cols]
            key = proj_t[pl.ds(256 + at, 16), cols]
            grad = att_grad_t[pl.ds(at, 16), cols]
            outs.append(
                (
                    dot(key, score_grad),
                    dot(score_grad, query, NT),
                    dot(probs[pix, head].astype(BF16), grad, NT),
                )
            )
        for (pix, head), got in zip(units, outs):
            at = pl.multiple_of(head * 16, 16)
            cols = pl.ds(pix * 128, 128)
            proj_grad_t[pl.ds(at, 16), cols] = got[0].astype(BF16)
            proj_grad_t[pl.ds(256 + at, 16), cols] = got[1].T.astype(BF16)
            proj_grad_t[pl.ds(512 + at, 16), cols] = got[2].T.astype(BF16)
        return carry

    lax.fori_loop(0, HEADS // BATCH, attend_back, 0)

    grad_t = proj_grad_t[...]
    first_t = first_in.T
    for part in range(3):
        qkv_grad = dot(first_t, grad_t[part * 256 : part * 256 + 256], NT)
        put(2 * part, slice(256, 384), qkv_grad[:, :128])
        put(2 * part + 1, slice(256, 384), qkv_grad[:, 128:])
    first_back = dot(grad_t, qkv_ref[...], ((0,), (1,)))
    grad = resid_grad + norm_back(normed_one, inverse_one, gain_first, first_back)
    grad = jnp.where(keep, grad, 0.0).astype(BF16)
    slot = iota((256, 256), 0)
    want = slot // 4 % 2 * 128 + slot // 8 * 4 + slot % 4
    grad_ref[...] = dot((iota((256, 256), 1) == want).astype(BF16), grad).astype(BF16)
    for at, sent_ref in enumerate(sent_refs):
        sent_ref[...] = terms_ref[at // 4, at % 4]


def core_sum_kernel(mine_ref, other_ref, out_ref):
    out_ref[...] = (mine_ref[...].astype(F32) + other_ref[...].astype(F32)).astype(BF16)


def x_sum_kernel(mine_ref, other_ref, one_ref, two_ref, three_ref, grad_ref, out_ref):
    total = mine_ref[...].astype(F32) + other_ref[...].astype(F32)
    total = total + one_ref[...].astype(F32)
    total = total + two_ref[...].astype(F32) + three_ref[...].astype(F32)
    out_ref[:, :, 0:384] = total.astype(BF16).reshape(32, 8, 384)
    out_ref[:, :, 384:640] = grad_ref[...].reshape(32, 8, 256)


def yz_sum_kernel(joint_ref, total_ref):
    total = jnp.sum(joint_ref[:, :, 0:384].astype(F32), axis=0).astype(BF16)
    total_ref[...] = jnp.broadcast_to(total[None], total_ref.shape)


def expand_kernel(joint_ref, match_ref, out_ref):
    for group in range(2):
        back = joint_ref[group * 16 : group * 16 + 16, :, 384:640].reshape(128, 256)
        out_ref[pl.ds(group * 256, 256), :] = dot(match_ref[group], back, TN).astype(BF16)


def spread_kernel(flip, held_ref, *refs):
    qkv_hbm, out_hbm, up_hbm, down_hbm, wide, narrow, sent = refs[-7:]
    core = lax.axis_index("c") ^ flip
    copies = []
    for pair in range(4):
        group = 2 * pair + core
        for lane in range(4):
            rows = slice(lane * 64, lane * 64 + 64)
            piece = held_ref[lane, pair].astype(F32)
            wide[pair, rows, :] = piece[:, :256]
            narrow[pair, rows, :] = piece[:, 256:]
        if pair < 2:
            far = up_hbm.at[:, pl.ds(pl.multiple_of(group * 256, 256), 256)]
        else:
            far = down_hbm.at[pl.ds(pl.multiple_of((group - 4) * 256, 256), 256), :]
        if pair < 3:
            near = qkv_hbm.at[:, pl.ds(pl.multiple_of(group * 128, 128), 128)]
        else:
            near = out_hbm.at[:, pl.ds(pl.multiple_of((group - 6) * 128, 128), 128)]
        for source, target, at in ((wide, far, 0), (narrow, near, 1)):
            copy = pltpu.make_async_copy(source.at[pair], target, sent.at[pair, at])
            copy.start()
            copies.append(copy)
    for copy in copies:
        copy.wait()


def spread(flip, held, *outs):
    shape = jax.ShapeDtypeStruct
    kept = pl.BlockSpec(memory_space=pl.ANY)
    return pl.pallas_call(
        functools.partial(spread_kernel, flip),
        out_shape=(
            shape((256, 768), F32),
            shape((256, 256), F32),
            shape((256, 1024), F32),
            shape((1024, 256), F32),
        ),
        in_specs=[pl.BlockSpec(memory_space=pltpu.VMEM)] + [kept] * len(outs),
        out_specs=[kept] * 4,
        scratch_shapes=[
            pltpu.VMEM((4, 256, 256), F32),
            pltpu.VMEM((4, 256, 128), F32),
            pltpu.SemaphoreType.DMA((4, 2)),
        ],
        input_output_aliases={at + 1: at for at in range(len(outs))},
        compiler_params=pltpu.CompilerParams(vmem_limit_bytes=VMEM_LIMIT),
        cost_estimate=pl.CostEstimate(flops=0, bytes_accessed=3000000, transcendentals=0),
    )(held, *outs)


def stay(array):
    return pltpu.with_memory_space_constraint(array, pltpu.HBM)


def run(kernel, out_shape, *args, scratch=(), held=(), cost=None):
    specs = [
        pl.BlockSpec(memory_space=pltpu.HBM if at in held else pltpu.VMEM)
        for at in range(len(args))
    ]
    args = [stay(array) if at in held else array for at, array in enumerate(args)]
    return pl.pallas_call(
        kernel,
        out_shape=out_shape,
        in_specs=specs,
        scratch_shapes=list(scratch),
        compiler_params=pltpu.CompilerParams(vmem_limit_bytes=VMEM_LIMIT),
        cost_estimate=cost
        and pl.CostEstimate(flops=0, bytes_accessed=cost, transcendentals=0),
    )(*args)


def shift(array, axis, size, by):
    return lax.ppermute(array, axis, [(at, (at + by) % size) for at in range(size)])


def per_device(
    features,
    cotangent,
    valid_dates,
    gain_first,
    qkv_weight,
    out_weight,
    gain_second,
    up_weight,
    down_weight,
):
    shape = jax.ShapeDtypeStruct
    width = features.shape[-1]
    scale = float(256 * 2 * 256) ** (-0.5)
    dates = ("y", "z")
    with jax.named_scope("compact"):
        send, match = run(
            compact_kernel,
            (shape((512, width), BF16), shape((2, 128, 256), BF16)),
            features.reshape(512, width),
            cotangent.reshape(512, width),
            valid_dates.T,
            held=(0, 1, 2),
            scratch=(
                pltpu.VMEM((512, width), BF16),
                pltpu.VMEM((512, width), BF16),
                pltpu.VMEM((8, 32), jnp.int32),
                pltpu.SemaphoreType.DMA((3,)),
            ),
        )
    with jax.named_scope("to_owner"):
        recv = lax.all_to_all(
            send.reshape(32, 16, width), dates, split_axis=0, concat_axis=0, tiled=True
        )
    piece = shape((256, 384), BF16)
    with jax.named_scope("layer"):
        grad, *terms = run(
            functools.partial(layer_kernel, scale),
            (shape((256, width), BF16),) + (piece,) * 8,
            recv.reshape(512, width),
            gain_first.reshape(1, width),
            qkv_weight,
            out_weight,
            gain_second.reshape(1, width),
            up_weight,
            down_weight,
            held=range(1, 7),
            scratch=(
                pltpu.VMEM((1, width), F32),
                pltpu.VMEM((256, 768), BF16),
                pltpu.VMEM((256, 256), BF16),
                pltpu.VMEM((1, width), F32),
                pltpu.VMEM((256, 1024), BF16),
                pltpu.VMEM((1024, 256), BF16),
                pltpu.SemaphoreType.DMA((6,)),
                pltpu.VMEM((2, HEADS, 128, 128), F32),
                pltpu.VMEM((768, 256), BF16),
                pltpu.VMEM((256, 256), BF16),
                pltpu.VMEM((256, 256), BF16),
                pltpu.VMEM((768, 256), BF16),
                pltpu.VMEM((2, 4, 256, 384), BF16),
            ),
        )
    with jax.named_scope("core_sum"):
        other = {by: shift(terms[4 + by], "c", 2, 1) for by in (3, 1, 2, 0)}
        slots = {by: run(core_sum_kernel, piece, terms[by], other[by]) for by in (3, 1, 2)}
    with jax.named_scope("x_sum"):
        got = [shift(slots[by], "x", 4, by) for by in (3, 1, 2)]
        joint = run(x_sum_kernel, shape((32, 8, 640), BF16), terms[0], other[0], *got, grad)
    with jax.named_scope("yz_sum"):
        joint = lax.all_to_all(joint, dates, split_axis=0, concat_axis=0, tiled=True)
        total = run(yz_sum_kernel, shape((8, 8, 384), BF16), joint)
    with jax.named_scope("z_gather"):
        part = lax.all_to_all(total, "z", split_axis=0, concat_axis=0, tiled=True)
    with jax.named_scope("yx_gather"):
        part = jnp.broadcast_to(part.reshape(1, 64, 384), (16, 64, 384))
        mine = lax.all_to_all(part, ("y", "x"), split_axis=0, concat_axis=0, tiled=True)
    with jax.named_scope("core_gather"):
        other = shift(mine, "c", 2, 1)
        joint, _ = lax.optimization_barrier((joint, mine))
    with jax.named_scope("expand"):
        feature_grad = run(
            expand_kernel, shape((512, width), BF16), joint, match, cost=1000000
        )
    with jax.named_scope("spread"):
        outs = spread(0, mine.reshape(4, 4, 64, 384))
        outs = spread(1, other.reshape(4, 4, 64, 384), *outs)
    return (feature_grad.reshape(features.shape), *outs)


def solution(mesh):
    fine = Mesh(mesh.devices.reshape(4, 8, 4, 2), ("y", "z", "x", "c"))
    dates, tiles = ("y", "z"), ("x", "c")
    in_specs = (
        P(tiles, None, dates, None),
        P(tiles, None, dates, None),
        P(tiles, dates),
        P(),
        P(),
        P(),
        P(),
        P(),
        P(),
    )
    out_specs = (P(tiles, None, dates, None), P(), P(), P(), P())
    return jax.shard_map(
        per_device, mesh=fine, in_specs=in_specs, out_specs=out_specs, check_vma=False
    )
```

```python
import functools

import jax
import jax.numpy as jnp
from jax import lax
from jax.experimental import pallas as pl
from jax.experimental.pallas import tpu as pltpu
from jax.sharding import Mesh
from jax.sharding import PartitionSpec as P

HEADS = 16
BATCH = 16
EPS = 1e-05
GELU_C = 0.7978845608028654
GELU_A = 0.044715
ABSENT = 2.0**100

F32 = jnp.float32
BF16 = jnp.bfloat16
VMEM_LIMIT = 48 * 1024 * 1024


def iota(shape, axis):
    return lax.broadcasted_iota(jnp.int32, shape, axis)


def dot(left, right, dims=((1,), (0,))):
    return lax.dot_general(left, right, (dims, ((), ())), preferred_element_type=F32)


TN = ((0,), (0,))
NT = ((1,), (1,))


def slot_matrix(valid, group):
    date = iota((8, 256), 1) % 8
    day = iota((8, 256), 0)
    held = valid.astype(F32)
    keep_all = dot(held, (day == date).astype(F32), TN)
    rank_all = dot(held, (day < date).astype(F32), TN)
    own = iota((32, 256), 0) == iota((32, 256), 1) // 16 + group * 16
    keep = jnp.sum(jnp.where(own, keep_all, 0.0), axis=0, keepdims=True)
    rank = jnp.sum(jnp.where(own, rank_all, 0.0), axis=0, keepdims=True)
    shape = (256, 256)
    row, col = iota(shape, 0), iota(shape, 1)
    match = (
        (row // 16 == col // 16)
        & ((row // 4) % 2 == (col // 8) % 2)
        & (rank == (row % 4).astype(F32))
        & (keep > 0.5)
    )
    return match.astype(F32)


def compact_kernel(feat_hbm, cot_hbm, valid_hbm, send_ref, match_ref, feat, cot, valid_ref, arrived):
    copies = [
        pltpu.make_async_copy(valid_hbm, valid_ref, arrived.at[0]),
        pltpu.make_async_copy(feat_hbm, feat, arrived.at[1]),
        pltpu.make_async_copy(cot_hbm, cot, arrived.at[2]),
    ]
    for copy in copies:
        copy.start()
    copies[0].wait()
    valid = valid_ref[...]
    is_feat = (iota((256, 1), 0) // 8) % 2 == 0
    picks = []
    for group in range(2):
        match = slot_matrix(valid, group)
        pick_feat = jnp.where(is_feat, match, 0.0).astype(BF16)
        pick_cot = jnp.where(is_feat, 0.0, match).astype(BF16)
        filled = jnp.sum(match, axis=1, keepdims=True) > 0.5
        match_ref[group] = match.reshape(16, 16, 256)[:, :8].reshape(128, 256).astype(BF16)
        picks.append((pick_feat, pick_cot, is_feat & jnp.logical_not(filled)))
    copies[1].wait()
    copies[2].wait()
    for group, (pick_feat, pick_cot, absent) in enumerate(picks):
        rows = pl.ds(group * 256, 256)
        got = dot(pick_feat, feat[rows, :]) + dot(pick_cot, cot[rows, :])
        send_ref[rows, :] = jnp.where(absent, ABSENT, got).astype(BF16)


def row_mean(values):
    return jnp.sum(values, axis=-1, keepdims=True) * (1.0 / values.shape[-1])


def norm_rows(hidden):
    centre = hidden - row_mean(hidden)
    inverse = lax.rsqrt(row_mean(centre * centre) + EPS)
    return centre * inverse, inverse


def norm_back(normed, inverse, gain, upstream):
    scaled = upstream * gain
    return inverse * (scaled - row_mean(scaled) - normed * row_mean(scaled * normed))


def layer_kernel(
    scale,
    recv_ref,
    gain_first_hbm,
    qkv_hbm,
    out_w_hbm,
    gain_second_hbm,
    up_hbm,
    down_hbm,
    grad_ref,
    *rest,
):
    (*sent_refs, gain_first_ref, qkv_ref, out_w_ref, gain_second_ref, up_ref, down_ref) = rest[:14]
    arrived, probs, proj_t, att_t, att_grad_t, proj_grad_t, terms_ref = rest[14:]
    pairs = (
        (qkv_hbm, qkv_ref),
        (gain_first_hbm, gain_first_ref),
        (out_w_hbm, out_w_ref),
        (gain_second_hbm, gain_second_ref),
        (up_hbm, up_ref),
        (down_hbm, down_ref),
    )
    copies = [
        pltpu.make_async_copy(held, ref, arrived.at[at]) for at, (held, ref) in enumerate(pairs)
    ]
    for copy in copies:
        copy.start()
    core = lax.axis_index("c")
    place = lax.axis_index("x")

    def put(group, columns, value):
        slot = lax.rem(group // 2 - place + 4, 4)
        terms_ref[(group % 2) ^ core, slot, :, columns] = (value * scale).astype(BF16)

    token = iota((256, 512), 0)
    target = (token % 128) // 4 * 16 + token // 128 * 4 + token % 4
    source = iota((256, 512), 1)
    recv = recv_ref[...]
    inputs = dot((source == target).astype(BF16), recv)
    upstream = dot((source == target + 8).astype(BF16), recv).astype(BF16)
    keep = inputs[:, 0:1] < 0.5 * ABSENT
    inputs = jnp.where(keep, inputs, 0.0)
    normed_one, inverse_one = norm_rows(inputs)
    copies[0].wait()
    copies[1].wait()
    gain_first = gain_first_ref[...]
    first_in = (normed_one * gain_first).astype(BF16)
    proj_t[...] = dot(qkv_ref[...], first_in, ((0,), (1,))).astype(BF16)

    def attend(batch, carry):
        units = [(pix, batch * BATCH + step) for step in range(BATCH) for pix in range(2)]
        scores, full = [], []
        for pix, head in units:
            at = pl.multiple_of(head * 16, 16)
            cols = pl.ds(pix * 128, 128)
            query = proj_t[pl.ds(at, 16), cols]
            key = proj_t[pl.ds(256 + at, 16), cols]
            scores.append(dot(key, query, TN))
        for (pix, head), score in zip(units, scores):
            score = jnp.where(keep[pix * 128 : pix * 128 + 128], score * 0.25, -1e30)
            powered = jnp.exp(score - jnp.max(score, axis=0, keepdims=True))
            full.append(powered * (1.0 / jnp.sum(powered, axis=0, keepdims=True)))
        for (pix, head), prob in zip(units, full):
            probs[pix, head] = prob
            at = pl.multiple_of(head * 16, 16)
            cols = pl.ds(pix * 128, 128)
            value = proj_t[pl.ds(512 + at, 16), cols]
            att_t[pl.ds(at, 16), cols] = dot(value, prob.astype(BF16)).astype(BF16)
        return carry

    lax.fori_loop(0, HEADS // BATCH, attend, 0)

    for copy in copies[2:]:
        copy.wait()
    gain_second = gain_second_ref[...]
    attended_t = att_t[...]
    out_w = out_w_ref[...]
    residual = inputs + dot(attended_t, out_w, TN)
    normed_two, inverse_two = norm_rows(residual)
    second_in = (normed_two * gain_second).astype(BF16)
    back = jnp.zeros((256, 256), F32)
    for part in range(4):
        cols = pl.ds(part * 256, 256)
        up_part = up_ref[:, cols]
        pre = dot(second_in, up_part)
        tangent = jnp.tanh(GELU_C * (pre + GELU_A * pre * pre * pre))
        activated = (0.5 * pre * (1.0 + tangent)).astype(BF16)
        slope = 0.5 * (1.0 + tangent) + 0.5 * pre * (1.0 - tangent * tangent) * GELU_C * (
            1.0 + 3.0 * GELU_A * pre * pre
        )
        put(4 + part, slice(0, 256), dot(activated, upstream, TN))
        hidden_grad = (dot(upstream, down_ref[cols, :], NT) * slope).astype(BF16)
        put(part, slice(0, 256), dot(second_in, hidden_grad, TN))
        back = back + dot(hidden_grad, up_part, NT)
    resid_grad = upstream.astype(F32) + norm_back(normed_two, inverse_two, gain_second, back)
    resid_half = resid_grad.astype(BF16)
    out_grad = dot(attended_t, resid_half)
    put(6, slice(256, 384), out_grad[:, :128])
    put(7, slice(256, 384), out_grad[:, 128:])
    att_grad_t[...] = dot(out_w, resid_half, NT).astype(BF16)

    def attend_back(batch, carry):
        units = [(pix, batch * BATCH + step) for step in range(BATCH) for pix in range(2)]
        prob_grads, score_grads, outs = [], [], []
        for pix, head in units:
            at = pl.multiple_of(head * 16, 16)
            cols = pl.ds(pix * 128, 128)
            value = proj_t[pl.ds(512 + at, 16), cols]
            prob_grads.append(dot(value, att_grad_t[pl.ds(at, 16), cols], TN))
        for (pix, head), prob_grad in zip(units, prob_grads):
            full = probs[pix, head]
            total = jnp.sum(full * prob_grad, axis=0, keepdims=True)
            score_grads.append((full * (prob_grad - total) * 0.25).astype(BF16))
        for (pix, head), score_grad in zip(units, score_grads):
            at = pl.multiple_of(head * 16, 16)
            cols = pl.ds(pix * 128, 128)
            query = proj_t[pl.ds(at, 16), cols]
            key = proj_t[pl.ds(256 + at, 16), cols]
            grad = att_grad_t[pl.ds(at, 16), cols]
            outs.append(
                (
                    dot(key, score_grad),
                    dot(score_grad, query, NT),
                    dot(probs[pix, head].astype(BF16), grad, NT),
                )
            )
        for (pix, head), got in zip(units, outs):
            at = pl.multiple_of(head * 16, 16)
            cols = pl.ds(pix * 128, 128)
            proj_grad_t[pl.ds(at, 16), cols] = got[0].astype(BF16)
            proj_grad_t[pl.ds(256 + at, 16), cols] = got[1].T.astype(BF16)
            proj_grad_t[pl.ds(512 + at, 16), cols] = got[2].T.astype(BF16)
        return carry

    lax.fori_loop(0, HEADS // BATCH, attend_back, 0)

    grad_t = proj_grad_t[...]
    first_t = first_in.T
    for part in range(3):
        qkv_grad = dot(first_t, grad_t[part * 256 : part * 256 + 256], NT)
        put(2 * part, slice(256, 384), qkv_grad[:, :128])
        put(2 * part + 1, slice(256, 384), qkv_grad[:, 128:])
    first_back = dot(grad_t, qkv_ref[...], ((0,), (1,)))
    grad = resid_grad + norm_back(normed_one, inverse_one, gain_first, first_back)
    grad = jnp.where(keep, grad, 0.0).astype(BF16)
    slot = iota((256, 256), 0)
    want = slot // 4 % 2 * 128 + slot // 8 * 4 + slot % 4
    grad_ref[...] = dot((iota((256, 256), 1) == want).astype(BF16), grad).astype(BF16)
    for at, sent_ref in enumerate(sent_refs):
        sent_ref[...] = terms_ref[at // 4, at % 4]


def core_sum_kernel(mine_ref, other_ref, out_ref):
    out_ref[...] = (mine_ref[...].astype(F32) + other_ref[...].astype(F32)).astype(BF16)


def x_sum_kernel(mine_ref, other_ref, one_ref, two_ref, three_ref, grad_ref, out_ref):
    total = mine_ref[...].astype(F32) + other_ref[...].astype(F32)
    total = total + one_ref[...].astype(F32)
    total = total + two_ref[...].astype(F32) + three_ref[...].astype(F32)
    out_ref[:, :, 0:384] = total.astype(BF16).reshape(32, 8, 384)
    out_ref[:, :, 384:640] = grad_ref[...].reshape(32, 8, 256)


def yz_sum_kernel(joint_ref, total_ref):
    total = jnp.sum(joint_ref[:, :, 0:384].astype(F32), axis=0).astype(BF16)
    total_ref[...] = jnp.broadcast_to(total[None], total_ref.shape)


def expand_kernel(joint_ref, match_ref, out_ref):
    for group in range(2):
        back = joint_ref[group * 16 : group * 16 + 16, :, 384:640].reshape(128, 256)
        out_ref[pl.ds(group * 256, 256), :] = dot(match_ref[group], back, TN).astype(BF16)


def spread_kernel(flip, held_ref, *refs):
    qkv_hbm, out_hbm, up_hbm, down_hbm, wide, narrow, sent = refs[-7:]
    core = lax.axis_index("c") ^ flip
    copies = []
    for pair in range(4):
        group = 2 * pair + core
        for lane in range(4):
            rows = slice(lane * 64, lane * 64 + 64)
            piece = held_ref[lane, pair].astype(F32)
            wide[pair, rows, :] = piece[:, :256]
            narrow[pair, rows, :] = piece[:, 256:]
        if pair < 2:
            far = up_hbm.at[:, pl.ds(pl.multiple_of(group * 256, 256), 256)]
        else:
            far = down_hbm.at[pl.ds(pl.multiple_of((group - 4) * 256, 256), 256), :]
        if pair < 3:
            near = qkv_hbm.at[:, pl.ds(pl.multiple_of(group * 128, 128), 128)]
        else:
            near = out_hbm.at[:, pl.ds(pl.multiple_of((group - 6) * 128, 128), 128)]
        for source, target, at in ((wide, far, 0), (narrow, near, 1)):
            copy = pltpu.make_async_copy(source.at[pair], target, sent.at[pair, at])
            copy.start()
            copies.append(copy)
    for copy in copies:
        copy.wait()


def spread(flip, held, *outs):
    shape = jax.ShapeDtypeStruct
    kept = pl.BlockSpec(memory_space=pl.ANY)
    return pl.pallas_call(
        functools.partial(spread_kernel, flip),
        out_shape=(
            shape((256, 768), F32),
            shape((256, 256), F32),
            shape((256, 1024), F32),
            shape((1024, 256), F32),
        ),
        in_specs=[pl.BlockSpec(memory_space=pltpu.VMEM)] + [kept] * len(outs),
        out_specs=[kept] * 4,
        scratch_shapes=[
            pltpu.VMEM((4, 256, 256), F32),
            pltpu.VMEM((4, 256, 128), F32),
            pltpu.SemaphoreType.DMA((4, 2)),
        ],
        input_output_aliases={at + 1: at for at in range(len(outs))},
        compiler_params=pltpu.CompilerParams(vmem_limit_bytes=VMEM_LIMIT),
        cost_estimate=pl.CostEstimate(flops=0, bytes_accessed=3000000, transcendentals=0),
    )(held, *outs)


def stay(array):
    return pltpu.with_memory_space_constraint(array, pltpu.HBM)


def run(kernel, out_shape, *args, scratch=(), held=(), cost=None):
    specs = [
        pl.BlockSpec(memory_space=pltpu.HBM if at in held else pltpu.VMEM)
        for at in range(len(args))
    ]
    args = [stay(array) if at in held else array for at, array in enumerate(args)]
    return pl.pallas_call(
        kernel,
        out_shape=out_shape,
        in_specs=specs,
        scratch_shapes=list(scratch),
        compiler_params=pltpu.CompilerParams(vmem_limit_bytes=VMEM_LIMIT),
        cost_estimate=cost
        and pl.CostEstimate(flops=0, bytes_accessed=cost, transcendentals=0),
    )(*args)


def shift(array, axis, size, by):
    return lax.ppermute(array, axis, [(at, (at + by) % size) for at in range(size)])


def per_device(
    features,
    cotangent,
    valid_dates,
    gain_first,
    qkv_weight,
    out_weight,
    gain_second,
    up_weight,
    down_weight,
):
    shape = jax.ShapeDtypeStruct
    width = features.shape[-1]
    scale = float(256 * 2 * 256) ** (-0.5)
    dates = ("y", "z")
    with jax.named_scope("compact"):
        send, match = run(
            compact_kernel,
            (shape((512, width), BF16), shape((2, 128, 256), BF16)),
            features.reshape(512, width),
            cotangent.reshape(512, width),
            valid_dates.T,
            held=(0, 1, 2),
            scratch=(
                pltpu.VMEM((512, width), BF16),
                pltpu.VMEM((512, width), BF16),
                pltpu.VMEM((8, 32), jnp.int32),
                pltpu.SemaphoreType.DMA((3,)),
            ),
        )
    with jax.named_scope("to_owner"):
        recv = lax.all_to_all(
            send.reshape(32, 16, width), dates, split_axis=0, concat_axis=0, tiled=True
        )
    piece = shape((256, 384), BF16)
    with jax.named_scope("layer"):
        grad, *terms = run(
            functools.partial(layer_kernel, scale),
            (shape((256, width), BF16),) + (piece,) * 8,
            recv.reshape(512, width),
            gain_first.reshape(1, width),
            qkv_weight,
            out_weight,
            gain_second.reshape(1, width),
            up_weight,
            down_weight,
            held=range(1, 7),
            scratch=(
                pltpu.VMEM((1, width), F32),
                pltpu.VMEM((256, 768), BF16),
                pltpu.VMEM((256, 256), BF16),
                pltpu.VMEM((1, width), F32),
                pltpu.VMEM((256, 1024), BF16),
                pltpu.VMEM((1024, 256), BF16),
                pltpu.SemaphoreType.DMA((6,)),
                pltpu.VMEM((2, HEADS, 128, 128), F32),
                pltpu.VMEM((768, 256), BF16),
                pltpu.VMEM((256, 256), BF16),
                pltpu.VMEM((256, 256), BF16),
                pltpu.VMEM((768, 256), BF16),
                pltpu.VMEM((2, 4, 256, 384), BF16),
            ),
        )
    with jax.named_scope("core_sum"):
        other = {by: shift(terms[4 + by], "c", 2, 1) for by in (2, 1, 3, 0)}
        slots = {by: run(core_sum_kernel, piece, terms[by], other[by]) for by in (2, 1, 3)}
    with jax.named_scope("x_sum"):
        got = [shift(slots[by], "x", 4, by) for by in (2, 1, 3)]
        joint = run(x_sum_kernel, shape((32, 8, 640), BF16), terms[0], other[0], *got, grad)
    with jax.named_scope("yz_sum"):
        joint = lax.all_to_all(joint, dates, split_axis=0, concat_axis=0, tiled=True)
        total = run(yz_sum_kernel, shape((8, 8, 384), BF16), joint)
    with jax.named_scope("z_gather"):
        part = lax.all_to_all(total, "z", split_axis=0, concat_axis=0, tiled=True)
    with jax.named_scope("yx_gather"):
        part = jnp.broadcast_to(part.reshape(1, 64, 384), (16, 64, 384))
        mine = lax.all_to_all(part, ("y", "x"), split_axis=0, concat_axis=0, tiled=True)
    with jax.named_scope("core_gather"):
        other = shift(mine, "c", 2, 1)
        joint, _ = lax.optimization_barrier((joint, mine))
    with jax.named_scope("expand"):
        feature_grad = run(
            expand_kernel, shape((512, width), BF16), joint, match, cost=1000000
        )
    with jax.named_scope("spread"):
        outs = spread(0, mine.reshape(4, 4, 64, 384))
        outs = spread(1, other.reshape(4, 4, 64, 384), *outs)
    return (feature_grad.reshape(features.shape), *outs)


def solution(mesh):
    fine = Mesh(mesh.devices.reshape(4, 8, 4, 2), ("y", "z", "x", "c"))
    dates, tiles = ("y", "z"), ("x", "c")
    in_specs = (
        P(tiles, None, dates, None),
        P(tiles, None, dates, None),
        P(tiles, dates),
        P(),
        P(),
        P(),
        P(),
        P(),
        P(),
    )
    out_specs = (P(tiles, None, dates, None), P(), P(), P(), P())
    return jax.shard_map(
        per_device, mesh=fine, in_specs=in_specs, out_specs=out_specs, check_vma=False
    )
```
